32 devices in a mesh: tm: 4 (over x, core), mesh: 8 (over z, y).
Axes of the slice: x: 2, y: 2, z: 4, core: 2. Of those that a mesh axis runs over, the one named last changes fastest.
Arguments:
- states: bfloat16 [32, 1024, 256], P('tm', 'mesh'), may hold values from -6 to 6
- increment: float32 [32, 1024, 256], P('tm', 'mesh'), may hold values from -6 to 6
- window_slots: int32 [8, 4], P('mesh'), may hold values from 0 to 2, as said below
- edge_weights: bfloat16 [2, 8, 4, 128, 128], P(None, 'mesh'), may hold values from -0.125 to 0.125
- inner_weight: bfloat16 [2, 256, 1024], replicated, may hold values from -0.375 to 0.375
- inner_bias: float32 [2, 1024], replicated, may hold values from -5 to 5
- outer_weight: bfloat16 [2, 1024, 256], replicated, may hold values from -0.1875 to 0.1875
Outputs:
- misfit: float32 [32, 1024, 256], P('tm', 'mesh')
- normal_product: float32 [32, 1024, 256], P('tm', 'mesh')
The draws below stay inside these ranges and needn't reach their ends.
Inputs may be any that keep to these rules, and one draw needn't show every extreme that they name: `window_slots`: slot 0 of a block's window is the block of the previous partition along mesh (cyclically), slot 1 the partition's own block, slot 2 the block of the next partition; every block's list names slot 0 and slot 2 at least once, and may name a slot twice.
All inputs are finite; a program needn't handle non-finite values.
Results may differ from the reference program's by a relative error of at most 0.007.
Values may be sent and summed in bfloat16 or wider, within the bound.
A program may use at most 64 MiB of HBM per device.

```python
import jax
import jax.numpy as jnp
from jax import lax

D = 256
HID = 1024
BLOCK = 128
FANOUT = 4
LAYERS = 2
BLK_DEV = 1
BLOCKS = 8
NODES = 1024
SUBWIN = 32


def draw_window_slots(key, part):
    key_values, key_rotate = jax.random.split(key)
    entries = jax.random.randint(key_values, (BLOCKS, FANOUT), 0, BLK_DEV + 2, dtype=jnp.int32)
    columns = jnp.arange(FANOUT, dtype=jnp.int32)[None, :]
    entries = jnp.where(columns == 0, jnp.int32(0), jnp.where(columns == 1, jnp.int32(BLK_DEV + 1), entries))
    rotation = jax.random.randint(key_rotate, (BLOCKS, 1), 0, FANOUT, dtype=jnp.int32)
    ordering = jnp.mod(columns + rotation, FANOUT).astype(jnp.int32)
    return jnp.take_along_axis(entries, ordering, axis=1)


def shard_levels(stream_key, shape, cuts, low, high):
    level = 1.0
    for position, shards_of in cuts:
        steps = jax.random.uniform(jax.random.fold_in(jax.random.fold_in(stream_key, 6), position), (shards_of,), jnp.float32, low / len(cuts), high / len(cuts))
        level = level * jnp.repeat(jnp.exp(steps), shape[position] // shards_of).reshape((-1,) + (1,) * (len(shape) - 1 - position))
    return level


def scatter_about(stream_key, dims, width, reach, cuts=(), held_as=jnp.bfloat16):
    gain = shard_levels(stream_key, dims, cuts, -0.22, 0.18) if cuts else 1.0
    drawn = jax.random.normal(stream_key, dims, jnp.float32) * width * gain
    return jnp.minimum(jnp.maximum(drawn, -reach), reach).astype(held_as)


def setup_inputs(seed: int = 0) -> dict:
    key_list = jax.random.split(jax.random.key(seed), 8)
    return {
        "states": scatter_about(key_list[0], (SUBWIN, NODES, D), 1.0, 6.0, ((0, 4), (1, 8))),
        "increment": scatter_about(key_list[1], (SUBWIN, NODES, D), 1.0, 6.0, ((0, 4), (1, 8)), jnp.float32),
        "window_slots": draw_window_slots(jax.random.fold_in(key_list[7], 71), 0),
        "edge_weights": scatter_about(key_list[3], (LAYERS, BLOCKS, FANOUT, BLOCK, BLOCK), (4 * FANOUT * BLOCK) ** -0.5, 0.125, ((1, 8),)),
        "inner_weight": scatter_about(key_list[4], (LAYERS, D, HID), D ** -0.5, 0.375),
        "inner_bias": scatter_about(key_list[5], (LAYERS, HID), 1.0, 5.0, (), jnp.float32),
        "outer_weight": scatter_about(key_list[6], (LAYERS, HID, D), HID ** -0.5, 0.1875),
    }


HALF_ROOT = 0.7071067811865476
DENSITY_NORM = 0.3989422804014327


def smooth_gate(values):
    return 0.5 * values * (1.0 + lax.erf(values * HALF_ROOT))


def smooth_slope(values):
    return 0.5 * (1.0 + lax.erf(values * HALF_ROOT)) + values * jnp.exp(-0.5 * values * values) * DENSITY_NORM


def block_targets(window_slots):
    block_count = window_slots.shape[0]
    block_ids = jnp.arange(block_count, dtype=jnp.int32)
    first_block = block_ids - block_ids % BLK_DEV
    return jnp.mod(first_block[:, None] + window_slots - 1, block_count).astype(jnp.int32)


def aggregate(source, targets, weights):
    block_view = source.astype(jnp.float32).reshape(BLOCKS, BLOCK, D)
    accumulated = jnp.zeros((BLOCKS, BLOCK, D), jnp.float32)
    for column in range(FANOUT):
        picked = block_view[targets[:, column]]
        accumulated = accumulated + jnp.einsum("bmn,bnd->bmd", weights[:, column].astype(jnp.float32), picked, precision=lax.Precision.HIGHEST)
    return accumulated.reshape(NODES, D)


def transpose_aggregate(source, targets, weights):
    block_view = source.astype(jnp.float32).reshape(BLOCKS, BLOCK, D)
    accumulated = jnp.zeros((BLOCKS, BLOCK, D), jnp.float32)
    for column in range(FANOUT):
        pieces = jnp.einsum("bmn,bmd->bnd", weights[:, column].astype(jnp.float32), block_view, precision=lax.Precision.HIGHEST)
        accumulated = accumulated + jax.ops.segment_sum(pieces, targets[:, column], num_segments=BLOCKS)
    return accumulated.reshape(NODES, D)


def linearize(state, targets, edge_weights, inner_weight, inner_bias, outer_weight):
    base_state = state
    slopes = []
    for layer_index in range(LAYERS):
        base_sum = base_state.astype(jnp.float32) + aggregate(base_state, targets, edge_weights[layer_index])
        activation = jnp.dot(base_sum.astype(jnp.bfloat16), inner_weight[layer_index], preferred_element_type=jnp.float32) + inner_bias[layer_index]
        slopes.append(smooth_slope(activation))
        if layer_index + 1 < LAYERS:
            gated = smooth_gate(activation).astype(jnp.bfloat16)
            base_state = (base_sum + jnp.dot(gated, outer_weight[layer_index], preferred_element_type=jnp.float32)).astype(jnp.bfloat16)
    return slopes


def reference(states, increment, window_slots, edge_weights, inner_weight, inner_bias, outer_weight):
    targets = block_targets(window_slots)

    def forward_one(stacked):
        state, source = stacked
        slopes = linearize(state, targets, edge_weights, inner_weight, inner_bias, outer_weight)
        tangent = source
        for layer_index in range(LAYERS):
            tangent_sum = tangent + aggregate(tangent.astype(jnp.bfloat16), targets, edge_weights[layer_index])
            lifted = (slopes[layer_index] * jnp.dot(tangent_sum.astype(jnp.bfloat16), inner_weight[layer_index], preferred_element_type=jnp.float32)).astype(jnp.bfloat16)
            tangent = tangent_sum + jnp.dot(lifted, outer_weight[layer_index], preferred_element_type=jnp.float32)
        return tangent

    images = lax.map(forward_one, (states, increment))
    misfit = jnp.concatenate([increment[:1], increment[1:] - images[:-1]], axis=0)
    following = jnp.concatenate([misfit[1:], jnp.zeros_like(misfit[:1])], axis=0)

    def adjoint_one(stacked):
        state, cotangent = stacked
        slopes = linearize(state, targets, edge_weights, inner_weight, inner_bias, outer_weight)
        current = cotangent
        for layer_index in range(LAYERS - 1, -1, -1):
            narrow = current.astype(jnp.bfloat16)
            spread = jnp.dot(narrow, outer_weight[layer_index].T, preferred_element_type=jnp.float32)
            pulled = (slopes[layer_index] * spread).astype(jnp.bfloat16)
            returned = current + jnp.dot(pulled, inner_weight[layer_index].T, preferred_element_type=jnp.float32)
            current = returned + transpose_aggregate(returned.astype(jnp.bfloat16), targets, edge_weights[layer_index])
        return current

    pulled_back = lax.map(adjoint_one, (states, following))
    return misfit, misfit - pulled_back
```

```python
import jax
import jax.numpy as jnp
from jax import lax
from jax.sharding import PartitionSpec as P

LAYERS = 2


HALF_ROOT = 0.7071067811865476
DENSITY_NORM = 0.3989422804014327


def shifted(value, axis, steps):
    count = lax.axis_size(axis)
    pairs = [(source, (source + steps) % count) for source in range(count)]
    return lax.ppermute(value, axis, pairs)


def extended(cells, sides, width):
    for axis, dim in sides:
        count = lax.axis_size(axis)
        head = lax.slice_in_dim(cells, 0, width, axis=dim)
        tail = lax.slice_in_dim(cells, cells.shape[dim] - width, cells.shape[dim], axis=dim)
        cells = jnp.concatenate(
            [
                lax.ppermute(tail, axis, [(i, (i + 1) % count) for i in range(count)]),
                cells,
                lax.ppermute(head, axis, [((i + 1) % count, i) for i in range(count)]),
            ],
            axis=dim,
        )
    return cells


def shifted_2(array, axis, by):
    count = lax.axis_size(axis)
    pairs = [(i, i + by) for i in range(count) if 0 <= i + by < count]
    return lax.ppermute(array, axis, pairs)


def smooth_gate(values):
    return 0.5 * values * (1.0 + lax.erf(values * HALF_ROOT))


def smooth_slope(values):
    return (
        0.5 * (1.0 + lax.erf(values * HALF_ROOT))
        + values * jnp.exp(-0.5 * values * values) * DENSITY_NORM
    )


def aggregate(window, window_slots, weights):
    windows, total_rows, features = window.shape
    blocks = weights.shape[0]
    block_rows = weights.shape[2]
    slots = total_rows // block_rows
    block_view = window.reshape(windows, slots, block_rows, features)
    chosen = (window_slots[:, :, None] == jnp.arange(slots, dtype=jnp.int32)).astype(jnp.float32)
    by_slot = jnp.einsum(
        "bkmn,bkw->bmwn", weights.astype(jnp.float32), chosen, precision=lax.Precision.HIGHEST
    ).astype(jnp.bfloat16)
    summed = jnp.einsum("bmwn,twnd->tbmd", by_slot, block_view, preferred_element_type=jnp.float32)
    return summed.reshape(windows, blocks * block_rows, features)


def transpose_aggregate(source, window_slots, weights):
    windows, node_rows, features = source.shape
    blocks = weights.shape[0]
    block_rows = weights.shape[2]
    block_view = source.reshape(windows, blocks, block_rows, features)
    pieces = jnp.einsum("bkmn,tbmd->tbknd", weights, block_view, preferred_element_type=jnp.float32)
    selector = (
        window_slots[:, :, None] == jnp.arange(blocks + 2, dtype=jnp.int32)[None, None, :]
    ).astype(jnp.float32)
    collected = jnp.einsum("tbknd,bkw->twnd", pieces, selector, precision=lax.Precision.HIGHEST)
    from_right = shifted(collected[:, 0].astype(jnp.bfloat16), "mesh", -1).astype(jnp.float32)
    from_left = shifted(collected[:, blocks + 1].astype(jnp.bfloat16), "mesh", 1).astype(
        jnp.float32
    )
    own_blocks = collected[:, 1 : blocks + 1]
    own_blocks = own_blocks.at[:, 0].add(from_left)
    own_blocks = own_blocks.at[:, blocks - 1].add(from_right)
    return own_blocks.reshape(windows, node_rows, features)


def forward_pass(
    linear_states, source_field, window_slots, edge_weights, inner_weight, inner_bias, outer_weight
):
    windows = linear_states.shape[0]
    block_rows = edge_weights.shape[-1]
    base_state = linear_states
    tangent = source_field
    slopes = []
    for layer_index in range(LAYERS):
        stacked = jnp.concatenate([base_state, tangent.astype(jnp.bfloat16)], axis=0)
        window = extended(stacked, (("mesh", 1),), block_rows)
        blended = aggregate(window, window_slots, edge_weights[layer_index])
        base_sum = base_state.astype(jnp.float32) + blended[:windows]
        tangent_sum = tangent + blended[windows:]
        activation = (
            jnp.einsum(
                "tnd,dh->tnh",
                base_sum.astype(jnp.bfloat16),
                inner_weight[layer_index],
                preferred_element_type=jnp.float32,
            )
            + inner_bias[layer_index]
        )
        derivative = smooth_slope(activation)
        slopes.append(derivative)
        lifted = (
            derivative
            * jnp.einsum(
                "tnd,dh->tnh",
                tangent_sum.astype(jnp.bfloat16),
                inner_weight[layer_index],
                preferred_element_type=jnp.float32,
            )
        ).astype(jnp.bfloat16)
        tangent = tangent_sum + jnp.einsum(
            "tnh,hd->tnd", lifted, outer_weight[layer_index], preferred_element_type=jnp.float32
        )
        if layer_index + 1 < LAYERS:
            gated = smooth_gate(activation).astype(jnp.bfloat16)
            base_state = (
                base_sum
                + jnp.einsum(
                    "tnh,hd->tnd",
                    gated,
                    outer_weight[layer_index],
                    preferred_element_type=jnp.float32,
                )
            ).astype(jnp.bfloat16)
    return (slopes, tangent)


def adjoint_pass(slopes, cotangent, window_slots, edge_weights, inner_weight, outer_weight):
    current = cotangent
    for layer_index in range(LAYERS - 1, -1, -1):
        narrow = current.astype(jnp.bfloat16)
        spread = jnp.einsum(
            "tnd,hd->tnh", narrow, outer_weight[layer_index], preferred_element_type=jnp.float32
        )
        pulled = (slopes[layer_index] * spread).astype(jnp.bfloat16)
        returned = current + jnp.einsum(
            "tnh,dh->tnd", pulled, inner_weight[layer_index], preferred_element_type=jnp.float32
        )
        current = returned + transpose_aggregate(
            returned.astype(jnp.bfloat16), window_slots, edge_weights[layer_index]
        )
    return current


def local_halo(states, increment, window_slots, edge_weights, inner_weight, inner_bias, outer_weight):
    windows = states.shape[0]
    kept_slopes, images = forward_pass(
        states, increment, window_slots, edge_weights, inner_weight, inner_bias, outer_weight
    )
    previous = shifted_2(images[windows - 1 :].astype(jnp.bfloat16), "tm", 1).astype(jnp.float32)
    misfit = increment - jnp.concatenate([previous, images[: windows - 1]], axis=0)
    following = shifted_2(misfit[:1].astype(jnp.bfloat16), "tm", -1).astype(jnp.float32)
    cotangent = jnp.concatenate([misfit[1:], following], axis=0)
    pulled_back = adjoint_pass(
        kept_slopes, cotangent, window_slots, edge_weights, inner_weight, outer_weight
    )
    normal = misfit - pulled_back
    return (misfit, normal)


def gathered_edges(window_slots, edge_weights):
    names = jnp.arange(3, dtype=jnp.int32)
    chosen = (window_slots[0][:, None] == names[None, :]).astype(jnp.float32)
    summed = jnp.einsum(
        "lkmn,ks->lmsn", edge_weights[:, 0].astype(jnp.float32), chosen, precision=lax.Precision.HIGHEST
    ).astype(jnp.bfloat16)
    layers, rows, slots, columns = summed.shape
    share = rows // lax.axis_size("tm")
    mine = lax.dynamic_slice_in_dim(summed, lax.axis_index("tm") * share, share, axis=1)
    part = lax.all_gather(mine, "mesh", axis=0)
    full = lax.all_gather(part, "tm", axis=2, tiled=True)
    return full.transpose(1, 0, 2, 3, 4).reshape(layers, full.shape[0], rows, slots * columns)


def whole_aggregate(field, matrices):
    blocks, rows, _ = matrices.shape
    view = field.reshape(blocks, rows, -1)
    window = jnp.concatenate([jnp.roll(view, 1, axis=0), view, jnp.roll(view, -1, axis=0)], axis=1)
    return jnp.einsum("bmk,bkd->bmd", matrices, window, preferred_element_type=jnp.float32).reshape(field.shape)


def whole_spread(field, matrices):
    blocks, rows, _ = matrices.shape
    view = field.reshape(blocks, rows, -1)
    pieces = jnp.einsum("bmk,bmd->bkd", matrices, view, preferred_element_type=jnp.float32)
    pieces = pieces.reshape(blocks, 3, rows, -1)
    total = jnp.roll(pieces[:, 0], -1, axis=0) + pieces[:, 1] + jnp.roll(pieces[:, 2], 1, axis=0)
    return total.reshape(field.shape)


def product(left, right):
    return jnp.dot(left, right, preferred_element_type=jnp.float32)


def local(states, increment, window_slots, edge_weights, inner_weight, inner_bias, outer_weight):
    windows = states.shape[0]
    parts = lax.axis_size("mesh")
    if windows != parts or edge_weights.shape[1] != 1:
        return local_halo(
            states, increment, window_slots, edge_weights, inner_weight, inner_bias, outer_weight
        )
    narrow = increment.astype(jnp.bfloat16)
    matrices = gathered_edges(window_slots, edge_weights)
    base = lax.all_to_all(states, "mesh", 0, 1, tiled=True)[0]
    tangent_in = lax.all_to_all(narrow, "mesh", 0, 1, tiled=True)[0]
    groups = lax.axis_size("tm")
    total = groups * parts
    later = lax.ppermute(tangent_in, ("tm", "mesh"), [(i + 1, i) for i in range(total - 1)])
    tangent = tangent_in.astype(jnp.float32)
    slopes = []
    for layer in range(LAYERS):
        base_sum = base.astype(jnp.float32) + whole_aggregate(base, matrices[layer])
        tangent_sum = tangent + whole_aggregate(tangent.astype(jnp.bfloat16), matrices[layer])
        pre = product(base_sum.astype(jnp.bfloat16), inner_weight[layer]) + inner_bias[layer]
        slope = smooth_slope(pre)
        slopes.append(slope)
        lifted = (slope * product(tangent_sum.astype(jnp.bfloat16), inner_weight[layer])).astype(jnp.bfloat16)
        tangent = tangent_sum + product(lifted, outer_weight[layer])
        if layer + 1 < LAYERS:
            base = (base_sum + product(smooth_gate(pre).astype(jnp.bfloat16), outer_weight[layer])).astype(jnp.bfloat16)
    mine = lax.axis_index("tm") * parts + lax.axis_index("mesh")
    current = jnp.where(mine == total - 1, 0.0, later.astype(jnp.float32) - tangent)
    change = (tangent - tangent_in.astype(jnp.float32)).astype(jnp.bfloat16)
    images = increment + lax.all_to_all(change[None], "mesh", 1, 0, tiled=True).astype(jnp.float32)
    for layer in range(LAYERS - 1, -1, -1):
        pulled = (
            slopes[layer]
            * jnp.einsum("nd,hd->nh", current.astype(jnp.bfloat16), outer_weight[layer], preferred_element_type=jnp.float32)
        ).astype(jnp.bfloat16)
        returned = current + jnp.einsum("nh,dh->nd", pulled, inner_weight[layer], preferred_element_type=jnp.float32)
        current = returned + whole_spread(returned.astype(jnp.bfloat16), matrices[layer])
    pulled_back = lax.all_to_all(current.astype(jnp.bfloat16)[None], "mesh", 1, 0, tiled=True)
    previous = shifted_2(images[windows - 1 :].astype(jnp.bfloat16), "tm", 1).astype(jnp.float32)
    misfit = increment - jnp.concatenate([previous, images[: windows - 1]], axis=0)
    return (misfit, misfit - pulled_back.astype(jnp.float32))


def solution(mesh):
    placed = (
        P("tm", "mesh", None),
        P("tm", "mesh", None),
        P("mesh", None),
        P(None, "mesh", None, None, None),
        P(),
        P(),
        P(),
    )
    return jax.shard_map(
        local,
        mesh=mesh,
        in_specs=placed,
        out_specs=(P("tm", "mesh", None), P("tm", "mesh", None)),
        check_vma=False,
    )
```

```python
import functools

import jax
import jax.numpy as jnp
from jax import lax
from jax.experimental import pallas as pl
from jax.experimental.pallas import tpu as pltpu
from jax.sharding import PartitionSpec as P

LAYERS = 2


HALF_ROOT = 0.7071067811865476
DENSITY_NORM = 0.3989422804014327


def shifted(value, axis, steps):
    count = lax.axis_size(axis)
    pairs = [(source, (source + steps) % count) for source in range(count)]
    return lax.ppermute(value, axis, pairs)


def extended(cells, sides, width):
    for axis, dim in sides:
        count = lax.axis_size(axis)
        head = lax.slice_in_dim(cells, 0, width, axis=dim)
        tail = lax.slice_in_dim(cells, cells.shape[dim] - width, cells.shape[dim], axis=dim)
        cells = jnp.concatenate(
            [
                lax.ppermute(tail, axis, [(i, (i + 1) % count) for i in range(count)]),
                cells,
                lax.ppermute(head, axis, [((i + 1) % count, i) for i in range(count)]),
            ],
            axis=dim,
        )
    return cells


def shifted_2(array, axis, by):
    count = lax.axis_size(axis)
    pairs = [(i, i + by) for i in range(count) if 0 <= i + by < count]
    return lax.ppermute(array, axis, pairs)


def smooth_gate(values):
    return 0.5 * values * (1.0 + lax.erf(values * HALF_ROOT))


def smooth_slope(values):
    return (
        0.5 * (1.0 + lax.erf(values * HALF_ROOT))
        + values * jnp.exp(-0.5 * values * values) * DENSITY_NORM
    )


def aggregate(window, window_slots, weights):
    windows, total_rows, features = window.shape
    blocks = weights.shape[0]
    block_rows = weights.shape[2]
    slots = total_rows // block_rows
    block_view = window.reshape(windows, slots, block_rows, features)
    chosen = (window_slots[:, :, None] == jnp.arange(slots, dtype=jnp.int32)).astype(jnp.float32)
    by_slot = jnp.einsum(
        "bkmn,bkw->bmwn", weights.astype(jnp.float32), chosen, precision=lax.Precision.HIGHEST
    ).astype(jnp.bfloat16)
    summed = jnp.einsum("bmwn,twnd->tbmd", by_slot, block_view, preferred_element_type=jnp.float32)
    return summed.reshape(windows, blocks * block_rows, features)


def transpose_aggregate(source, window_slots, weights):
    windows, node_rows, features = source.shape
    blocks = weights.shape[0]
    block_rows = weights.shape[2]
    block_view = source.reshape(windows, blocks, block_rows, features)
    pieces = jnp.einsum("bkmn,tbmd->tbknd", weights, block_view, preferred_element_type=jnp.float32)
    selector = (
        window_slots[:, :, None] == jnp.arange(blocks + 2, dtype=jnp.int32)[None, None, :]
    ).astype(jnp.float32)
    collected = jnp.einsum("tbknd,bkw->twnd", pieces, selector, precision=lax.Precision.HIGHEST)
    from_right = shifted(collected[:, 0].astype(jnp.bfloat16), "mesh", -1).astype(jnp.float32)
    from_left = shifted(collected[:, blocks + 1].astype(jnp.bfloat16), "mesh", 1).astype(
        jnp.float32
    )
    own_blocks = collected[:, 1 : blocks + 1]
    own_blocks = own_blocks.at[:, 0].add(from_left)
    own_blocks = own_blocks.at[:, blocks - 1].add(from_right)
    return own_blocks.reshape(windows, node_rows, features)


def forward_pass(
    linear_states, source_field, window_slots, edge_weights, inner_weight, inner_bias, outer_weight
):
    windows = linear_states.shape[0]
    block_rows = edge_weights.shape[-1]
    base_state = linear_states
    tangent = source_field
    slopes = []
    for layer_index in range(LAYERS):
        stacked = jnp.concatenate([base_state, tangent.astype(jnp.bfloat16)], axis=0)
        window = extended(stacked, (("mesh", 1),), block_rows)
        blended = aggregate(window, window_slots, edge_weights[layer_index])
        base_sum = base_state.astype(jnp.float32) + blended[:windows]
        tangent_sum = tangent + blended[windows:]
        activation = (
            jnp.einsum(
                "tnd,dh->tnh",
                base_sum.astype(jnp.bfloat16),
                inner_weight[layer_index],
                preferred_element_type=jnp.float32,
            )
            + inner_bias[layer_index]
        )
        derivative = smooth_slope(activation)
        slopes.append(derivative)
        lifted = (
            derivative
            * jnp.einsum(
                "tnd,dh->tnh",
                tangent_sum.astype(jnp.bfloat16),
                inner_weight[layer_index],
                preferred_element_type=jnp.float32,
            )
        ).astype(jnp.bfloat16)
        tangent = tangent_sum + jnp.einsum(
            "tnh,hd->tnd", lifted, outer_weight[layer_index], preferred_element_type=jnp.float32
        )
        if layer_index + 1 < LAYERS:
            gated = smooth_gate(activation).astype(jnp.bfloat16)
            base_state = (
                base_sum
                + jnp.einsum(
                    "tnh,hd->tnd",
                    gated,
                    outer_weight[layer_index],
                    preferred_element_type=jnp.float32,
                )
            ).astype(jnp.bfloat16)
    return (slopes, tangent)


def adjoint_pass(slopes, cotangent, window_slots, edge_weights, inner_weight, outer_weight):
    current = cotangent
    for layer_index in range(LAYERS - 1, -1, -1):
        narrow = current.astype(jnp.bfloat16)
        spread = jnp.einsum(
            "tnd,hd->tnh", narrow, outer_weight[layer_index], preferred_element_type=jnp.float32
        )
        pulled = (slopes[layer_index] * spread).astype(jnp.bfloat16)
        returned = current + jnp.einsum(
            "tnh,dh->tnd", pulled, inner_weight[layer_index], preferred_element_type=jnp.float32
        )
        current = returned + transpose_aggregate(
            returned.astype(jnp.bfloat16), window_slots, edge_weights[layer_index]
        )
    return current


def local_halo(states, increment, window_slots, edge_weights, inner_weight, inner_bias, outer_weight):
    windows = states.shape[0]
    kept_slopes, images = forward_pass(
        states, increment, window_slots, edge_weights, inner_weight, inner_bias, outer_weight
    )
    previous = shifted_2(images[windows - 1 :].astype(jnp.bfloat16), "tm", 1).astype(jnp.float32)
    misfit = increment - jnp.concatenate([previous, images[: windows - 1]], axis=0)
    following = shifted_2(misfit[:1].astype(jnp.bfloat16), "tm", -1).astype(jnp.float32)
    cotangent = jnp.concatenate([misfit[1:], following], axis=0)
    pulled_back = adjoint_pass(
        kept_slopes, cotangent, window_slots, edge_weights, inner_weight, outer_weight
    )
    normal = misfit - pulled_back
    return (misfit, normal)


def edge_share(window_slots, edge_weights):
    names = jnp.arange(3, dtype=jnp.int32)
    chosen = (window_slots[0][:, None] == names[None, :]).astype(jnp.float32)
    summed = jnp.einsum(
        "lkmn,ks->lmsn", edge_weights[:, 0].astype(jnp.float32), chosen, precision=lax.Precision.HIGHEST
    ).astype(jnp.bfloat16)
    layers, rows, slots, columns = summed.shape
    share = rows // lax.axis_size("tm")
    mine = lax.dynamic_slice_in_dim(summed, lax.axis_index("tm") * share, share, axis=1)
    return mine.reshape(layers, share, slots * columns)


def dot(left, right, dims):
    return lax.dot_general(left, right, (dims, ((), ())), preferred_element_type=jnp.float32)


NN = ((1,), (0,))
NT = ((1,), (1,))
TN = ((0,), (0,))
PAIR = 2


def whole_kernel(
    parts, states, narrow, increment, share, inner_weight, inner_bias, outer_weight, misfit, normal,
    edges, base, tangent_in, later, base_next, tangent_mid, tangent_low, slopes, image, cotangent, returned,
    returned_low, outgoing, image_in, adjoint_in,
    edge_send, edge_recv, state_send, state_recv, inc_send, inc_recv, tm_send, tm_recv, shift_send, shift_recv,
    image_send, image_recv, adjoint_send, adjoint_recv,
):
    group, me = lax.axis_index("tm"), lax.axis_index("mesh")
    groups = lax.axis_size("tm")
    last = parts - 1
    layers = inner_weight.shape[0]
    rows, features = base.shape[1], base.shape[2]
    group_next, group_prev = lax.rem(group + 1, groups), lax.rem(group + groups - 1, groups)
    across = lax.rem(group + 2, groups)
    beside = group + 1 - 2 * lax.rem(group, 2)
    beside_across = lax.rem(beside + 2, groups)

    def peer(step):
        return lax.rem(me + step, parts)

    barrier = pltpu.get_barrier_semaphore()

    def greet(g, m):
        pl.semaphore_signal(barrier, inc=1, device_id={"tm": g, "mesh": m}, device_id_type=pl.DeviceIdType.MESH)

    for step in range(1, parts):
        greet(group, peer(step))
    greet(across, me)
    greet(beside, me)
    greet(group_prev, last)

    @pl.when(me == last)
    def _():
        greet(group_next, 0)

    pl.semaphore_wait(
        barrier, parts + 1 + jnp.where(me == last, parts, 0) + jnp.where(me == 0, 1, 0)
    )

    def remote(src, dst, send, recv, g, m):
        return pltpu.make_async_remote_copy(
            src_ref=src, dst_ref=dst, send_sem=send, recv_sem=recv,
            device_id={"tm": g, "mesh": m}, device_id_type=pl.DeviceIdType.MESH,
        )

    edge_copies = [
        remote(share, edges.at[group, me], edge_send.at[d], edge_recv.at[d], group, peer(d)) for d in range(1, parts)
    ]
    state_copies = [
        remote(states.at[peer(d)], base.at[me], state_send.at[d], state_recv.at[d], group, peer(d))
        for d in range(1, parts)
    ]
    inc_copies = [
        remote(narrow.at[peer(d)], tangent_in.at[me], inc_send.at[d], inc_recv.at[d], group, peer(d))
        for d in range(1, parts)
    ]
    for copy in edge_copies + state_copies + inc_copies:
        copy.start()
    edges[group, me] = share[...]
    base[me] = states[me]
    tangent_in[me] = narrow[me]
    for copy in edge_copies:
        copy.wait_recv()
    first = remote(edges.at[group], edges.at[group], tm_send.at[0], tm_recv.at[0], across, me)
    first.start()
    second = remote(edges.at[group], edges.at[group], tm_send.at[1], tm_recv.at[1], beside, me)
    second.start()
    first.wait_recv()
    third = remote(edges.at[across], edges.at[across], tm_send.at[2], tm_recv.at[2], beside, me)
    third.start()
    second.wait_recv()
    third.wait_recv()
    for copy in state_copies:
        copy.wait_recv()

    def matrix(layer, block):
        return edges[:, block, layer].reshape(rows, -1)

    def aggregated(field, layer, block):
        window = jnp.concatenate(
            [field[lax.rem(block + last, parts)], field[block], field[lax.rem(block + 1, parts)]], axis=0
        )
        return dot(matrix(layer, block), window, NN)

    def summed(field, wide, layer, start):
        parts_of = [wide[start + i].astype(jnp.float32) + aggregated(field, layer, start + i) for i in range(PAIR)]
        return jnp.concatenate(parts_of, axis=0)

    def over_pairs(body):
        def step(index, carry):
            body(index * PAIR)
            return carry

        lax.fori_loop(0, parts // PAIR, step, 0)

    for layer in range(layers):
        field = base if layer == 0 else base_next

        def base_step(start, layer=layer, field=field):
            total = summed(field, field, layer, start)
            pre = dot(total.astype(jnp.bfloat16), inner_weight[layer], NN) + inner_bias[layer][None, :]
            phi = 0.5 * (1.0 + lax.erf(pre * HALF_ROOT))
            slopes[layer, pl.ds(start * rows, PAIR * rows)] = (
                phi + pre * jnp.exp(-0.5 * pre * pre) * DENSITY_NORM
            )
            if layer + 1 < layers:
                after = total + dot((pre * phi).astype(jnp.bfloat16), outer_weight[layer], NN)
                base_next[pl.ds(start, PAIR)] = after.astype(jnp.bfloat16).reshape(PAIR, rows, features)

        over_pairs(base_step)

    for copy in inc_copies:
        copy.wait_recv()
    low_group = jnp.where(me == 0, group_prev, group)
    shift = remote(tangent_in, later, shift_send.at[0], shift_recv.at[0], low_group, lax.rem(me + last, parts))
    shift.start()

    for layer in range(layers):
        field = tangent_in if layer == 0 else tangent_low
        wide = tangent_in if layer == 0 else tangent_mid

        def tangent_step(start, layer=layer, field=field, wide=wide):
            total = summed(field, wide, layer, start)
            lifted = (
                slopes[layer, pl.ds(start * rows, PAIR * rows)]
                * dot(total.astype(jnp.bfloat16), inner_weight[layer], NN)
            ).astype(jnp.bfloat16)
            after = (total + dot(lifted, outer_weight[layer], NN)).reshape(PAIR, rows, features)
            if layer + 1 < layers:
                tangent_mid[pl.ds(start, PAIR)] = after
                tangent_low[pl.ds(start, PAIR)] = after.astype(jnp.bfloat16)
            else:
                cotangent[pl.ds(start, PAIR)] = after
                image[pl.ds(start, PAIR)] = after.astype(jnp.bfloat16)

        over_pairs(tangent_step)

    slot = peer(1)
    own_group = jnp.where(me == last, group_next, group)
    image_copies = [
        remote(image.at[peer(d)], image_in.at[slot], image_send.at[d], image_recv.at[slot], own_group, peer(d))
        for d in range(parts)
    ]
    kept = pltpu.make_async_copy(image.at[me], image_in.at[slot], image_recv.at[slot])
    for copy in image_copies[1:]:
        copy.start()

    @pl.when(me == last)
    def _():
        image_copies[0].start()

    @pl.when(me != last)
    def _():
        kept.start()

    shift.wait_recv()
    final = jnp.logical_and(me == last, group == groups - 1)
    keep = jnp.where(final, 0.0, 1.0)

    def cotangent_step(start):
        here = pl.ds(start, PAIR)
        cotangent[here] = (later[here].astype(jnp.float32) - cotangent[here]) * keep

    over_pairs(cotangent_step)

    adjoint_copies = [
        remote(outgoing.at[peer(d)], adjoint_in.at[me], adjoint_send.at[d], adjoint_recv.at[d], group, peer(d))
        for d in range(1, parts)
    ]
    for layer in range(layers - 1, -1, -1):

        def adjoint_step(start, layer=layer):
            here = pl.ds(start, PAIR)
            current = cotangent[here].reshape(PAIR * rows, features)
            pulled = (
                slopes[layer, pl.ds(start * rows, PAIR * rows)]
                * dot(current.astype(jnp.bfloat16), outer_weight[layer], NT)
            ).astype(jnp.bfloat16)
            back = (current + dot(pulled, inner_weight[layer], NT)).reshape(PAIR, rows, features)
            returned[here] = back
            returned_low[here] = back.astype(jnp.bfloat16)

        over_pairs(adjoint_step)

        def spread_step(start, layer=layer):
            for i in range(PAIR):
                block = start + i
                above, below = lax.rem(block + 1, parts), lax.rem(block + last, parts)
                stack = jnp.concatenate(
                    [
                        matrix(layer, above)[:, :rows],
                        matrix(layer, block)[:, rows : 2 * rows],
                        matrix(layer, below)[:, 2 * rows :],
                    ],
                    axis=0,
                )
                window = jnp.concatenate([returned_low[above], returned_low[block], returned_low[below]], axis=0)
                after = returned[block] + dot(stack, window, TN)
                if layer > 0:
                    cotangent[block] = after
                else:
                    outgoing[block] = after.astype(jnp.bfloat16)

        over_pairs(spread_step)

    for copy in adjoint_copies:
        copy.start()
    adjoint_in[me] = outgoing[me]

    for s in range(parts):
        remote(image.at[0], image_in.at[s], image_send.at[0], image_recv.at[s], group, peer(1)).wait_recv()
        value = image_in[s].astype(jnp.float32)
        if s == 0:
            value = value * jnp.where(group == 0, 0.0, 1.0)
        misfit[s] = increment[s] - value
    for copy in adjoint_copies:
        copy.wait_recv()
    for s in range(parts):
        normal[s] = misfit[s] - adjoint_in[s].astype(jnp.float32)

    for copy in edge_copies + state_copies + inc_copies + [first, second, third, shift] + image_copies[1:]:
        copy.wait_send()
    for copy in adjoint_copies:
        copy.wait_send()

    @pl.when(me == last)
    def _():
        image_copies[0].wait_send()


def local(states, increment, window_slots, edge_weights, inner_weight, inner_bias, outer_weight):
    windows, rows, features = states.shape
    parts = lax.axis_size("mesh")
    groups = lax.axis_size("tm")
    layers, hidden = inner_bias.shape
    if windows != parts or edge_weights.shape[1] != 1 or groups != 4 or parts % PAIR:
        return local_halo(
            states, increment, window_slots, edge_weights, inner_weight, inner_bias, outer_weight
        )
    share = edge_share(window_slots, edge_weights)
    narrow = increment.astype(jnp.bfloat16)
    low = pltpu.VMEM((parts, rows, features), jnp.bfloat16)
    wide = pltpu.VMEM((parts, rows, features), jnp.float32)
    sems = pltpu.SemaphoreType.DMA
    vmem = pl.BlockSpec(memory_space=pltpu.VMEM)
    out = jax.ShapeDtypeStruct(increment.shape, jnp.float32)
    return pl.pallas_call(
        functools.partial(whole_kernel, parts),
        out_shape=(out, out),
        in_specs=[vmem] * 7,
        out_specs=(vmem, vmem),
        scratch_shapes=[
            pltpu.VMEM((groups, parts) + share.shape, jnp.bfloat16),
            low, low, low, low,
            wide, low,
            pltpu.VMEM((layers, parts * rows, hidden), jnp.float32),
            low, wide, wide,
            low, low, low, low,
            sems((parts,)), sems((parts,)), sems((parts,)), sems((parts,)), sems((parts,)), sems((parts,)),
            sems((3,)), sems((3,)), sems((1,)), sems((1,)),
            sems((parts,)), sems((parts,)), sems((parts,)), sems((parts,)),
        ],
        compiler_params=pltpu.CompilerParams(
            collective_id=0, has_side_effects=True, vmem_limit_bytes=48 * 1024 * 1024
        ),
    )(states, narrow, increment, share, inner_weight, inner_bias, outer_weight)


def solution(mesh):
    placed = (
        P("tm", "mesh", None),
        P("tm", "mesh", None),
        P("mesh", None),
        P(None, "mesh", None, None, None),
        P(),
        P(),
        P(),
    )
    return jax.shard_map(
        local,
        mesh=mesh,
        in_specs=placed,
        out_specs=(P("tm", "mesh", None), P("tm", "mesh", None)),
        check_vma=False,
    )
```

```python
import functools

import jax
import jax.numpy as jnp
from jax import lax
from jax.experimental import pallas as pl
from jax.experimental.pallas import tpu as pltpu
from jax.sharding import PartitionSpec as P

LAYERS = 2


HALF_ROOT = 0.7071067811865476
DENSITY_NORM = 0.3989422804014327


def shifted(value, axis, steps):
    count = lax.axis_size(axis)
    pairs = [(source, (source + steps) % count) for source in range(count)]
    return lax.ppermute(value, axis, pairs)


def extended(cells, sides, width):
    for axis, dim in sides:
        count = lax.axis_size(axis)
        head = lax.slice_in_dim(cells, 0, width, axis=dim)
        tail = lax.slice_in_dim(cells, cells.shape[dim] - width, cells.shape[dim], axis=dim)
        cells = jnp.concatenate(
            [
                lax.ppermute(tail, axis, [(i, (i + 1) % count) for i in range(count)]),
                cells,
                lax.ppermute(head, axis, [((i + 1) % count, i) for i in range(count)]),
            ],
            axis=dim,
        )
    return cells


def shifted_2(array, axis, by):
    count = lax.axis_size(axis)
    pairs = [(i, i + by) for i in range(count) if 0 <= i + by < count]
    return lax.ppermute(array, axis, pairs)


def smooth_gate(values):
    return 0.5 * values * (1.0 + lax.erf(values * HALF_ROOT))


def smooth_slope(values):
    return (
        0.5 * (1.0 + lax.erf(values * HALF_ROOT))
        + values * jnp.exp(-0.5 * values * values) * DENSITY_NORM
    )


def aggregate(window, window_slots, weights):
    windows, total_rows, features = window.shape
    blocks = weights.shape[0]
    block_rows = weights.shape[2]
    slots = total_rows // block_rows
    block_view = window.reshape(windows, slots, block_rows, features)
    chosen = (window_slots[:, :, None] == jnp.arange(slots, dtype=jnp.int32)).astype(jnp.float32)
    by_slot = jnp.einsum(
        "bkmn,bkw->bmwn", weights.astype(jnp.float32), chosen, precision=lax.Precision.HIGHEST
    ).astype(jnp.bfloat16)
    summed = jnp.einsum("bmwn,twnd->tbmd", by_slot, block_view, preferred_element_type=jnp.float32)
    return summed.reshape(windows, blocks * block_rows, features)


def transpose_aggregate(source, window_slots, weights):
    windows, node_rows, features = source.shape
    blocks = weights.shape[0]
    block_rows = weights.shape[2]
    block_view = source.reshape(windows, blocks, block_rows, features)
    pieces = jnp.einsum("bkmn,tbmd->tbknd", weights, block_view, preferred_element_type=jnp.float32)
    selector = (
        window_slots[:, :, None] == jnp.arange(blocks + 2, dtype=jnp.int32)[None, None, :]
    ).astype(jnp.float32)
    collected = jnp.einsum("tbknd,bkw->twnd", pieces, selector, precision=lax.Precision.HIGHEST)
    from_right = shifted(collected[:, 0].astype(jnp.bfloat16), "mesh", -1).astype(jnp.float32)
    from_left = shifted(collected[:, blocks + 1].astype(jnp.bfloat16), "mesh", 1).astype(
        jnp.float32
    )
    own_blocks = collected[:, 1 : blocks + 1]
    own_blocks = own_blocks.at[:, 0].add(from_left)
    own_blocks = own_blocks.at[:, blocks - 1].add(from_right)
    return own_blocks.reshape(windows, node_rows, features)


def forward_pass(
    linear_states, source_field, window_slots, edge_weights, inner_weight, inner_bias, outer_weight
):
    windows = linear_states.shape[0]
    block_rows = edge_weights.shape[-1]
    base_state = linear_states
    tangent = source_field
    slopes = []
    for layer_index in range(LAYERS):
        stacked = jnp.concatenate([base_state, tangent.astype(jnp.bfloat16)], axis=0)
        window = extended(stacked, (("mesh", 1),), block_rows)
        blended = aggregate(window, window_slots, edge_weights[layer_index])
        base_sum = base_state.astype(jnp.float32) + blended[:windows]
        tangent_sum = tangent + blended[windows:]
        activation = (
            jnp.einsum(
                "tnd,dh->tnh",
                base_sum.astype(jnp.bfloat16),
                inner_weight[layer_index],
                preferred_element_type=jnp.float32,
            )
            + inner_bias[layer_index]
        )
        derivative = smooth_slope(activation)
        slopes.append(derivative)
        lifted = (
            derivative
            * jnp.einsum(
                "tnd,dh->tnh",
                tangent_sum.astype(jnp.bfloat16),
                inner_weight[layer_index],
                preferred_element_type=jnp.float32,
            )
        ).astype(jnp.bfloat16)
        tangent = tangent_sum + jnp.einsum(
            "tnh,hd->tnd", lifted, outer_weight[layer_index], preferred_element_type=jnp.float32
        )
        if layer_index + 1 < LAYERS:
            gated = smooth_gate(activation).astype(jnp.bfloat16)
            base_state = (
                base_sum
                + jnp.einsum(
                    "tnh,hd->tnd",
                    gated,
                    outer_weight[layer_index],
                    preferred_element_type=jnp.float32,
                )
            ).astype(jnp.bfloat16)
    return (slopes, tangent)


def adjoint_pass(slopes, cotangent, window_slots, edge_weights, inner_weight, outer_weight):
    current = cotangent
    for layer_index in range(LAYERS - 1, -1, -1):
        narrow = current.astype(jnp.bfloat16)
        spread = jnp.einsum(
            "tnd,hd->tnh", narrow, outer_weight[layer_index], preferred_element_type=jnp.float32
        )
        pulled = (slopes[layer_index] * spread).astype(jnp.bfloat16)
        returned = current + jnp.einsum(
            "tnh,dh->tnd", pulled, inner_weight[layer_index], preferred_element_type=jnp.float32
        )
        current = returned + transpose_aggregate(
            returned.astype(jnp.bfloat16), window_slots, edge_weights[layer_index]
        )
    return current


def local_halo(states, increment, window_slots, edge_weights, inner_weight, inner_bias, outer_weight):
    windows = states.shape[0]
    kept_slopes, images = forward_pass(
        states, increment, window_slots, edge_weights, inner_weight, inner_bias, outer_weight
    )
    previous = shifted_2(images[windows - 1 :].astype(jnp.bfloat16), "tm", 1).astype(jnp.float32)
    misfit = increment - jnp.concatenate([previous, images[: windows - 1]], axis=0)
    following = shifted_2(misfit[:1].astype(jnp.bfloat16), "tm", -1).astype(jnp.float32)
    cotangent = jnp.concatenate([misfit[1:], following], axis=0)
    pulled_back = adjoint_pass(
        kept_slopes, cotangent, window_slots, edge_weights, inner_weight, outer_weight
    )
    normal = misfit - pulled_back
    return (misfit, normal)


def edge_share(window_slots, edge_weights):
    names = jnp.arange(3, dtype=jnp.int32)
    chosen = (window_slots[0][:, None] == names[None, :]).astype(jnp.float32)
    summed = jnp.einsum(
        "lkmn,ks->lmsn", edge_weights[:, 0].astype(jnp.float32), chosen, precision=lax.Precision.HIGHEST
    ).astype(jnp.bfloat16)
    layers, rows, slots, columns = summed.shape
    share = rows // lax.axis_size("tm")
    mine = lax.dynamic_slice_in_dim(summed, lax.axis_index("tm") * share, share, axis=1)
    return mine.reshape(layers, share, slots * columns)


def dot(left, right, dims):
    return lax.dot_general(left, right, (dims, ((), ())), preferred_element_type=jnp.float32)


NN = ((1,), (0,))
NT = ((1,), (1,))
TN = ((0,), (0,))
PAIR = 2


def whole_kernel(
    parts, states, increment, share, inner_hbm, inner_bias, outer_hbm, image_in, adjoint_in,
    inner_weight, outer_weight, wide_in, narrow, edges, base, tangent_in, later, base_next, tangent_mid, tangent_low, slopes, image, cotangent, returned,
    returned_low, outgoing,
    edge_send, edge_recv, state_send, state_recv, inc_send, inc_recv, tm_send, tm_recv, shift_send, shift_recv,
    image_send, image_recv, adjoint_send, adjoint_recv, local_sem,
):
    group, me = lax.axis_index("tm"), lax.axis_index("mesh")
    groups = lax.axis_size("tm")
    last = parts - 1
    layers = inner_weight.shape[0]
    rows, features = base.shape[1], base.shape[2]
    group_next, group_prev = lax.rem(group + 1, groups), lax.rem(group + groups - 1, groups)
    across = lax.rem(group + 2, groups)
    beside = group + 1 - 2 * lax.rem(group, 2)
    beside_across = lax.rem(beside + 2, groups)

    pairs = parts // 2
    high, side = me // 2, lax.rem(me, 2)

    def window_of(g, m):
        order = jnp.where(lax.rem(m, 2) == 0, m // 2, parts - 1 - m // 2)
        return jnp.where(lax.rem(g, 2) == 0, order, last - order)

    def holder_of(g, w):
        order = jnp.where(lax.rem(g, 2) == 0, w, last - w)
        return jnp.where(order < pairs, 2 * order, 2 * (last - order) + 1)

    window = window_of(group, me)
    prev_last, next_first = holder_of(group_prev, last), holder_of(group_next, 0)

    def peer(step):
        return lax.rem(me + step, parts)

    barrier = pltpu.get_barrier_semaphore()

    def greet(g, m):
        pl.semaphore_signal(barrier, inc=1, device_id={"tm": g, "mesh": m}, device_id_type=pl.DeviceIdType.MESH)

    for step in range(1, parts):
        greet(group, peer(step))
    greet(across, me)
    greet(beside, me)
    greet(group_prev, prev_last)

    @pl.when(window == last)
    def _():
        greet(group_next, next_first)

    pl.semaphore_wait(
        barrier, parts + 1 + jnp.where(window == last, parts, 0) + jnp.where(window == 0, 1, 0)
    )

    def remote(src, dst, send, recv, g, m):
        return pltpu.make_async_remote_copy(
            src_ref=src, dst_ref=dst, send_sem=send, recv_sem=recv,
            device_id={"tm": g, "mesh": m}, device_id_type=pl.DeviceIdType.MESH,
        )

    edge_copies = [
        remote(share, edges.at[group, side, high], edge_send.at[d], edge_recv.at[d], group, peer(2 * d))
        for d in range(1, pairs)
    ]
    state_copies = [
        remote(states.at[window_of(group, peer(d))], base.at[me], state_send.at[d], state_recv.at[d], group, peer(d))
        for d in range(1, parts)
    ]
    inc_copies = [
        remote(narrow.at[window_of(group, peer(d))], tangent_in.at[me], inc_send.at[d], inc_recv.at[d], group, peer(d))
        for d in range(1, parts)
    ]
    fetch = pltpu.make_async_copy(increment, wide_in, local_sem.at[0])
    loads = [
        pltpu.make_async_copy(inner_hbm, inner_weight, local_sem.at[1]),
        pltpu.make_async_copy(outer_hbm, outer_weight, local_sem.at[2]),
        pltpu.make_async_copy(states.at[window], base.at[me], local_sem.at[3]),
    ]
    fetch.start()
    for copy in edge_copies + state_copies:
        copy.start()
    fetch.wait()
    narrow[...] = wide_in[...].astype(jnp.bfloat16)
    for copy in inc_copies + loads:
        copy.start()
    edges[group, side, high] = share[...]
    tangent_in[me] = narrow[window]
    for copy in edge_copies:
        copy.wait_recv()
    aside = remote(
        edges.at[group, side], edges.at[group, side], edge_send.at[0], edge_recv.at[0], group, me + 1 - 2 * side
    )
    aside.start()
    aside.wait_recv()
    first = remote(edges.at[group], edges.at[group], tm_send.at[0], tm_recv.at[0], across, me)
    first.start()
    second = remote(edges.at[group], edges.at[group], tm_send.at[1], tm_recv.at[1], beside, me)
    second.start()
    first.wait_recv()
    third = remote(edges.at[across], edges.at[across], tm_send.at[2], tm_recv.at[2], beside, me)
    third.start()
    second.wait_recv()
    third.wait_recv()
    for copy in loads:
        copy.wait()
    for copy in state_copies:
        copy.wait_recv()

    def matrix(layer, block):
        return edges[:, lax.rem(block, 2), block // 2, layer].reshape(rows, -1)

    def aggregated(field, layer, block):
        window = jnp.concatenate(
            [field[lax.rem(block + last, parts)], field[block], field[lax.rem(block + 1, parts)]], axis=0
        )
        return dot(matrix(layer, block), window, NN)

    def summed(field, wide, layer, start):
        parts_of = [wide[start + i].astype(jnp.float32) + aggregated(field, layer, start + i) for i in range(PAIR)]
        return jnp.concatenate(parts_of, axis=0)

    def over_pairs(body):
        def step(index, carry):
            body(index * PAIR)
            return carry

        lax.fori_loop(0, parts // PAIR, step, 0)

    for layer in range(layers):
        field = base if layer == 0 else base_next

        def base_step(start, layer=layer, field=field):
            total = summed(field, field, layer, start)
            pre = dot(total.astype(jnp.bfloat16), inner_weight[layer], NN) + inner_bias[layer][None, :]
            phi = 0.5 * (1.0 + lax.erf(pre * HALF_ROOT))
            slopes[layer, pl.ds(start * rows, PAIR * rows)] = (
                phi + pre * jnp.exp(-0.5 * pre * pre) * DENSITY_NORM
            )
            if layer + 1 < layers:
                after = total + dot((pre * phi).astype(jnp.bfloat16), outer_weight[layer], NN)
                base_next[pl.ds(start, PAIR)] = after.astype(jnp.bfloat16).reshape(PAIR, rows, features)

        over_pairs(base_step)

    for copy in inc_copies:
        copy.wait_recv()
    low_group = jnp.where(window == 0, group_prev, group)
    low_me = jnp.where(window == 0, prev_last, holder_of(group, lax.rem(window + last, parts)))
    shift = remote(tangent_in, later, shift_send.at[0], shift_recv.at[0], low_group, low_me)
    shift.start()

    for layer in range(layers):
        field = tangent_in if layer == 0 else tangent_low
        wide = tangent_in if layer == 0 else tangent_mid

        def tangent_step(start, layer=layer, field=field, wide=wide):
            total = summed(field, wide, layer, start)
            lifted = (
                slopes[layer, pl.ds(start * rows, PAIR * rows)]
                * dot(total.astype(jnp.bfloat16), inner_weight[layer], NN)
            ).astype(jnp.bfloat16)
            after = (total + dot(lifted, outer_weight[layer], NN)).reshape(PAIR, rows, features)
            if layer + 1 < layers:
                tangent_mid[pl.ds(start, PAIR)] = after
                tangent_low[pl.ds(start, PAIR)] = after.astype(jnp.bfloat16)
            else:
                cotangent[pl.ds(start, PAIR)] = after
                image[pl.ds(start, PAIR)] = after.astype(jnp.bfloat16)

        over_pairs(tangent_step)

    slot = lax.rem(window + 1, parts)
    own_group = jnp.where(window == last, group_next, group)
    image_copies = [
        remote(image.at[peer(d)], image_in.at[slot], image_send.at[d], image_recv.at[slot], own_group, peer(d))
        for d in range(parts)
    ]
    kept = pltpu.make_async_copy(image.at[me], image_in.at[slot], image_recv.at[slot])
    for copy in image_copies[1:]:
        copy.start()

    @pl.when(window == last)
    def _():
        image_copies[0].start()

    @pl.when(window != last)
    def _():
        kept.start()

    shift.wait_recv()
    final = jnp.logical_and(window == last, group == groups - 1)
    keep = jnp.where(final, 0.0, 1.0)

    def cotangent_step(start):
        here = pl.ds(start, PAIR)
        cotangent[here] = (later[here].astype(jnp.float32) - cotangent[here]) * keep

    over_pairs(cotangent_step)

    adjoint_copies = [
        remote(outgoing.at[peer(d)], adjoint_in.at[window], adjoint_send.at[d], adjoint_recv.at[d], group, peer(d))
        for d in range(1, parts)
    ]
    for layer in range(layers - 1, -1, -1):

        def adjoint_step(start, layer=layer):
            here = pl.ds(start, PAIR)
            current = cotangent[here].reshape(PAIR * rows, features)
            pulled = (
                slopes[layer, pl.ds(start * rows, PAIR * rows)]
                * dot(current.astype(jnp.bfloat16), outer_weight[layer], NT)
            ).astype(jnp.bfloat16)
            back = (current + dot(pulled, inner_weight[layer], NT)).reshape(PAIR, rows, features)
            returned[here] = back
            returned_low[here] = back.astype(jnp.bfloat16)

        over_pairs(adjoint_step)

        def spread_step(start, layer=layer):
            for i in range(PAIR):
                block = start + i
                above, below = lax.rem(block + 1, parts), lax.rem(block + last, parts)
                stack = jnp.concatenate(
                    [
                        matrix(layer, above)[:, :rows],
                        matrix(layer, block)[:, rows : 2 * rows],
                        matrix(layer, below)[:, 2 * rows :],
                    ],
                    axis=0,
                )
                window = jnp.concatenate([returned_low[above], returned_low[block], returned_low[below]], axis=0)
                after = returned[block] + dot(stack, window, TN)
                if layer > 0:
                    cotangent[block] = after
                else:
                    outgoing[block] = after.astype(jnp.bfloat16)

        over_pairs(spread_step)

    for copy in adjoint_copies:
        copy.start()
    own = pltpu.make_async_copy(outgoing.at[me], adjoint_in.at[window], local_sem.at[4])
    own.start()
    for s in range(parts):
        remote(image.at[0], image_in.at[s], image_send.at[0], image_recv.at[s], group, peer(1)).wait_recv()
    for copy in adjoint_copies:
        copy.wait_recv()
    own.wait()

    for copy in edge_copies + state_copies + inc_copies + [aside, first, second, third, shift] + image_copies[1:]:
        copy.wait_send()
    for copy in adjoint_copies:
        copy.wait_send()

    @pl.when(window == last)
    def _():
        image_copies[0].wait_send()


def local(states, increment, window_slots, edge_weights, inner_weight, inner_bias, outer_weight):
    windows, rows, features = states.shape
    parts = lax.axis_size("mesh")
    groups = lax.axis_size("tm")
    layers, hidden = inner_bias.shape
    if windows != parts or edge_weights.shape[1] != 1 or groups != 4 or parts % PAIR:
        return local_halo(
            states, increment, window_slots, edge_weights, inner_weight, inner_bias, outer_weight
        )
    share = edge_share(window_slots, edge_weights)
    low = pltpu.VMEM((parts, rows, features), jnp.bfloat16)
    wide = pltpu.VMEM((parts, rows, features), jnp.float32)
    sems = pltpu.SemaphoreType.DMA
    vmem, anywhere = pl.BlockSpec(memory_space=pltpu.VMEM), pl.BlockSpec(memory_space=pl.ANY)
    out = jax.ShapeDtypeStruct(increment.shape, jnp.bfloat16)
    image, adjoint = pl.pallas_call(
        functools.partial(whole_kernel, parts),
        out_shape=(out, out),
        in_specs=[anywhere, anywhere, vmem, anywhere, vmem, anywhere],
        out_specs=(anywhere, anywhere),
        scratch_shapes=[
            pltpu.VMEM(inner_weight.shape, jnp.bfloat16),
            pltpu.VMEM(outer_weight.shape, jnp.bfloat16),
            wide, low,
            pltpu.VMEM((groups, 2, parts // 2) + share.shape, jnp.bfloat16),
            low, low, low, low,
            wide, low,
            pltpu.VMEM((layers, parts * rows, hidden), jnp.float32),
            low, wide, wide,
            low, low,
            sems((parts,)), sems((parts,)), sems((parts,)), sems((parts,)), sems((parts,)), sems((parts,)),
            sems((3,)), sems((3,)), sems((1,)), sems((1,)),
            sems((parts,)), sems((parts,)), sems((parts,)), sems((parts,)), sems((5,)),
        ],
        compiler_params=pltpu.CompilerParams(
            collective_id=0, has_side_effects=True, vmem_limit_bytes=56 * 1024 * 1024
        ),
    )(states, increment, share, inner_weight, inner_bias, outer_weight)
    first = jnp.logical_and(lax.axis_index("tm") == 0, jnp.arange(windows)[:, None, None] == 0)
    misfit = increment - jnp.where(first, 0.0, image.astype(jnp.float32))
    return misfit, misfit - adjoint.astype(jnp.float32)


def solution(mesh):
    placed = (
        P("tm", "mesh", None),
        P("tm", "mesh", None),
        P("mesh", None),
        P(None, "mesh", None, None, None),
        P(),
        P(),
        P(),
    )
    return jax.shard_map(
        local,
        mesh=mesh,
        in_specs=placed,
        out_specs=(P("tm", "mesh", None), P("tm", "mesh", None)),
        check_vma=False,
    )
```

```python
import functools

import jax
import jax.numpy as jnp
from jax import lax
from jax.experimental import pallas as pl
from jax.experimental.pallas import tpu as pltpu
from jax.sharding import PartitionSpec as P

LAYERS = 2


HALF_ROOT = 0.7071067811865476
DENSITY_NORM = 0.3989422804014327


def shifted(value, axis, steps):
    count = lax.axis_size(axis)
    pairs = [(source, (source + steps) % count) for source in range(count)]
    return lax.ppermute(value, axis, pairs)


def extended(cells, sides, width):
    for axis, dim in sides:
        count = lax.axis_size(axis)
        head = lax.slice_in_dim(cells, 0, width, axis=dim)
        tail = lax.slice_in_dim(cells, cells.shape[dim] - width, cells.shape[dim], axis=dim)
        cells = jnp.concatenate(
            [
                lax.ppermute(tail, axis, [(i, (i + 1) % count) for i in range(count)]),
                cells,
                lax.ppermute(head, axis, [((i + 1) % count, i) for i in range(count)]),
            ],
            axis=dim,
        )
    return cells


def shifted_2(array, axis, by):
    count = lax.axis_size(axis)
    pairs = [(i, i + by) for i in range(count) if 0 <= i + by < count]
    return lax.ppermute(array, axis, pairs)


def smooth_gate(values):
    return 0.5 * values * (1.0 + lax.erf(values * HALF_ROOT))


def smooth_slope(values):
    return (
        0.5 * (1.0 + lax.erf(values * HALF_ROOT))
        + values * jnp.exp(-0.5 * values * values) * DENSITY_NORM
    )


def aggregate(window, window_slots, weights):
    windows, total_rows, features = window.shape
    blocks = weights.shape[0]
    block_rows = weights.shape[2]
    slots = total_rows // block_rows
    block_view = window.reshape(windows, slots, block_rows, features)
    chosen = (window_slots[:, :, None] == jnp.arange(slots, dtype=jnp.int32)).astype(jnp.float32)
    by_slot = jnp.einsum(
        "bkmn,bkw->bmwn", weights.astype(jnp.float32), chosen, precision=lax.Precision.HIGHEST
    ).astype(jnp.bfloat16)
    summed = jnp.einsum("bmwn,twnd->tbmd", by_slot, block_view, preferred_element_type=jnp.float32)
    return summed.reshape(windows, blocks * block_rows, features)


def transpose_aggregate(source, window_slots, weights):
    windows, node_rows, features = source.shape
    blocks = weights.shape[0]
    block_rows = weights.shape[2]
    block_view = source.reshape(windows, blocks, block_rows, features)
    pieces = jnp.einsum("bkmn,tbmd->tbknd", weights, block_view, preferred_element_type=jnp.float32)
    selector = (
        window_slots[:, :, None] == jnp.arange(blocks + 2, dtype=jnp.int32)[None, None, :]
    ).astype(jnp.float32)
    collected = jnp.einsum("tbknd,bkw->twnd", pieces, selector, precision=lax.Precision.HIGHEST)
    from_right = shifted(collected[:, 0].astype(jnp.bfloat16), "mesh", -1).astype(jnp.float32)
    from_left = shifted(collected[:, blocks + 1].astype(jnp.bfloat16), "mesh", 1).astype(
        jnp.float32
    )
    own_blocks = collected[:, 1 : blocks + 1]
    own_blocks = own_blocks.at[:, 0].add(from_left)
    own_blocks = own_blocks.at[:, blocks - 1].add(from_right)
    return own_blocks.reshape(windows, node_rows, features)


def forward_pass(
    linear_states, source_field, window_slots, edge_weights, inner_weight, inner_bias, outer_weight
):
    windows = linear_states.shape[0]
    block_rows = edge_weights.shape[-1]
    base_state = linear_states
    tangent = source_field
    slopes = []
    for layer_index in range(LAYERS):
        stacked = jnp.concatenate([base_state, tangent.astype(jnp.bfloat16)], axis=0)
        window = extended(stacked, (("mesh", 1),), block_rows)
        blended = aggregate(window, window_slots, edge_weights[layer_index])
        base_sum = base_state.astype(jnp.float32) + blended[:windows]
        tangent_sum = tangent + blended[windows:]
        activation = (
            jnp.einsum(
                "tnd,dh->tnh",
                base_sum.astype(jnp.bfloat16),
                inner_weight[layer_index],
                preferred_element_type=jnp.float32,
            )
            + inner_bias[layer_index]
        )
        derivative = smooth_slope(activation)
        slopes.append(derivative)
        lifted = (
            derivative
            * jnp.einsum(
                "tnd,dh->tnh",
                tangent_sum.astype(jnp.bfloat16),
                inner_weight[layer_index],
                preferred_element_type=jnp.float32,
            )
        ).astype(jnp.bfloat16)
        tangent = tangent_sum + jnp.einsum(
            "tnh,hd->tnd", lifted, outer_weight[layer_index], preferred_element_type=jnp.float32
        )
        if layer_index + 1 < LAYERS:
            gated = smooth_gate(activation).astype(jnp.bfloat16)
            base_state = (
                base_sum
                + jnp.einsum(
                    "tnh,hd->tnd",
                    gated,
                    outer_weight[layer_index],
                    preferred_element_type=jnp.float32,
                )
            ).astype(jnp.bfloat16)
    return (slopes, tangent)


def adjoint_pass(slopes, cotangent, window_slots, edge_weights, inner_weight, outer_weight):
    current = cotangent
    for layer_index in range(LAYERS - 1, -1, -1):
        narrow = current.astype(jnp.bfloat16)
        spread = jnp.einsum(
            "tnd,hd->tnh", narrow, outer_weight[layer_index], preferred_element_type=jnp.float32
        )
        pulled = (slopes[layer_index] * spread).astype(jnp.bfloat16)
        returned = current + jnp.einsum(
            "tnh,dh->tnd", pulled, inner_weight[layer_index], preferred_element_type=jnp.float32
        )
        current = returned + transpose_aggregate(
            returned.astype(jnp.bfloat16), window_slots, edge_weights[layer_index]
        )
    return current


def local_halo(states, increment, window_slots, edge_weights, inner_weight, inner_bias, outer_weight):
    windows = states.shape[0]
    kept_slopes, images = forward_pass(
        states, increment, window_slots, edge_weights, inner_weight, inner_bias, outer_weight
    )
    previous = shifted_2(images[windows - 1 :].astype(jnp.bfloat16), "tm", 1).astype(jnp.float32)
    misfit = increment - jnp.concatenate([previous, images[: windows - 1]], axis=0)
    following = shifted_2(misfit[:1].astype(jnp.bfloat16), "tm", -1).astype(jnp.float32)
    cotangent = jnp.concatenate([misfit[1:], following], axis=0)
    pulled_back = adjoint_pass(
        kept_slopes, cotangent, window_slots, edge_weights, inner_weight, outer_weight
    )
    normal = misfit - pulled_back
    return (misfit, normal)


def edge_share(window_slots, edge_weights):
    names = jnp.arange(3, dtype=jnp.int32)
    chosen = (window_slots[0][:, None] == names[None, :]).astype(jnp.float32)
    summed = jnp.einsum(
        "lkmn,ks->lmsn", edge_weights[:, 0].astype(jnp.float32), chosen, precision=lax.Precision.HIGHEST
    ).astype(jnp.bfloat16)
    layers, rows, slots, columns = summed.shape
    share = rows // lax.axis_size("tm")
    mine = lax.dynamic_slice_in_dim(summed, lax.axis_index("tm") * share, share, axis=1)
    return mine.reshape(layers, share, slots * columns)


def dot(left, right, dims):
    return lax.dot_general(left, right, (dims, ((), ())), preferred_element_type=jnp.float32)


NN = ((1,), (0,))
NT = ((1,), (1,))
TN = ((0,), (0,))
PAIR = 2


def whole_kernel(
    parts, states, increment, share, inner_hbm, inner_bias, outer_hbm, image_in, adjoint_in,
    inner_weight, outer_weight, wide_in, narrow, edges, base, tangent_in, later, base_next, tangent_mid, tangent_low, slopes, image, cotangent, returned,
    returned_low, outgoing,
    edge_send, edge_recv, state_send, state_recv, inc_send, inc_recv, tm_send, tm_recv, shift_send, shift_recv,
    image_send, image_recv, adjoint_send, adjoint_recv, local_sem,
):
    group, me = lax.axis_index("tm"), lax.axis_index("mesh")
    groups = lax.axis_size("tm")
    last = parts - 1
    layers = inner_weight.shape[0]
    rows, features = base.shape[1], base.shape[2]
    group_next, group_prev = lax.rem(group + 1, groups), lax.rem(group + groups - 1, groups)
    across = lax.rem(group + 2, groups)
    beside = group + 1 - 2 * lax.rem(group, 2)
    beside_across = lax.rem(beside + 2, groups)

    pairs = parts // 2
    high, side = me // 2, lax.rem(me, 2)

    def window_of(g, m):
        order = jnp.where(lax.rem(m, 2) == 0, m // 2, parts - 1 - m // 2)
        return jnp.where(lax.rem(g, 2) == 0, order, last - order)

    def holder_of(g, w):
        order = jnp.where(lax.rem(g, 2) == 0, w, last - w)
        return jnp.where(order < pairs, 2 * order, 2 * (last - order) + 1)

    window = window_of(group, me)
    prev_last, next_first = holder_of(group_prev, last), holder_of(group_next, 0)

    def peer(step):
        return lax.rem(me + step, parts)

    barrier = pltpu.get_barrier_semaphore()

    def greet(g, m):
        pl.semaphore_signal(barrier, inc=1, device_id={"tm": g, "mesh": m}, device_id_type=pl.DeviceIdType.MESH)

    for step in range(1, parts):
        greet(group, peer(step))
    greet(across, me)
    greet(beside, me)
    greet(group_prev, prev_last)

    @pl.when(window == last)
    def _():
        greet(group_next, next_first)

    pl.semaphore_wait(
        barrier, parts + 1 + jnp.where(window == last, parts, 0) + jnp.where(window == 0, 1, 0)
    )

    def remote(src, dst, send, recv, g, m):
        return pltpu.make_async_remote_copy(
            src_ref=src, dst_ref=dst, send_sem=send, recv_sem=recv,
            device_id={"tm": g, "mesh": m}, device_id_type=pl.DeviceIdType.MESH,
        )

    edge_copies = [
        remote(share, edges.at[group, side, high], edge_send.at[d], edge_recv.at[d], group, peer(2 * d))
        for d in range(1, pairs)
    ]
    state_copies = [
        remote(states.at[window_of(group, peer(d))], base.at[me], state_send.at[d], state_recv.at[d], group, peer(d))
        for d in range(1, parts)
    ]
    inc_copies = [
        remote(narrow.at[window_of(group, peer(d))], tangent_in.at[me], inc_send.at[d], inc_recv.at[d], group, peer(d))
        for d in range(1, parts)
    ]
    fetch = pltpu.make_async_copy(increment, wide_in, local_sem.at[0])
    loads = [
        pltpu.make_async_copy(inner_hbm, inner_weight, local_sem.at[1]),
        pltpu.make_async_copy(outer_hbm, outer_weight, local_sem.at[2]),
        pltpu.make_async_copy(states.at[window], base.at[me], local_sem.at[3]),
    ]
    fetch.start()
    for copy in edge_copies + state_copies:
        copy.start()
    fetch.wait()
    narrow[...] = wide_in[...].astype(jnp.bfloat16)
    for copy in inc_copies + loads:
        copy.start()
    edges[group, side, high] = share[...]
    tangent_in[me] = narrow[window]
    for copy in edge_copies:
        copy.wait_recv()
    aside = remote(
        edges.at[group, side], edges.at[group, side], edge_send.at[0], edge_recv.at[0], group, me + 1 - 2 * side
    )
    aside.start()
    aside.wait_recv()
    first = remote(edges.at[group], edges.at[group], tm_send.at[0], tm_recv.at[0], across, me)
    first.start()
    second = remote(edges.at[group], edges.at[group], tm_send.at[1], tm_recv.at[1], beside, me)
    second.start()
    first.wait_recv()
    third = remote(edges.at[across], edges.at[across], tm_send.at[2], tm_recv.at[2], beside, me)
    third.start()
    second.wait_recv()
    third.wait_recv()
    for copy in loads:
        copy.wait()
    for copy in state_copies:
        copy.wait_recv()

    def matrix(layer, block):
        return edges[:, lax.rem(block, 2), block // 2, layer].reshape(rows, -1)

    def aggregated(field, layer, block):
        window = jnp.concatenate(
            [field[lax.rem(block + last, parts)], field[block], field[lax.rem(block + 1, parts)]], axis=0
        )
        return dot(matrix(layer, block), window, NN)

    def summed(field, wide, layer, start):
        parts_of = [wide[start + i].astype(jnp.float32) + aggregated(field, layer, start + i) for i in range(PAIR)]
        return jnp.concatenate(parts_of, axis=0)

    def over_pairs(body):
        def step(index, carry):
            body(lax.rem(index + me // PAIR, parts // PAIR) * PAIR)
            return carry

        lax.fori_loop(0, parts // PAIR, step, 0)

    for layer in range(layers):
        field = base if layer == 0 else base_next

        def base_step(start, layer=layer, field=field):
            total = summed(field, field, layer, start)
            pre = dot(total.astype(jnp.bfloat16), inner_weight[layer], NN) + inner_bias[layer][None, :]
            phi = 0.5 * (1.0 + lax.erf(pre * HALF_ROOT))
            slopes[layer, pl.ds(start * rows, PAIR * rows)] = (
                phi + pre * jnp.exp(-0.5 * pre * pre) * DENSITY_NORM
            )
            if layer + 1 < layers:
                after = total + dot((pre * phi).astype(jnp.bfloat16), outer_weight[layer], NN)
                base_next[pl.ds(start, PAIR)] = after.astype(jnp.bfloat16).reshape(PAIR, rows, features)

        over_pairs(base_step)

    for copy in inc_copies:
        copy.wait_recv()
    low_group = jnp.where(window == 0, group_prev, group)
    low_me = jnp.where(window == 0, prev_last, holder_of(group, lax.rem(window + last, parts)))
    shift = remote(tangent_in, later, shift_send.at[0], shift_recv.at[0], low_group, low_me)
    shift.start()

    slot = lax.rem(window + 1, parts)
    own_group = jnp.where(window == last, group_next, group)
    image_copies = [
        remote(image.at[peer(d)], image_in.at[slot], image_send.at[d], image_recv.at[slot], own_group, peer(d))
        for d in range(parts)
    ]
    kept = pltpu.make_async_copy(image.at[me], image_in.at[slot], image_recv.at[slot])

    def send_image(block):
        step = lax.rem(block - me + parts, parts)
        stays = jnp.logical_and(step == 0, window != last)

        @pl.when(stays)
        def _():
            kept.start()

        @pl.when(jnp.logical_not(stays))
        def _():
            remote(
                image.at[block], image_in.at[slot], image_send.at[step], image_recv.at[slot], own_group, block
            ).start()

    for layer in range(layers):
        field = tangent_in if layer == 0 else tangent_low
        wide = tangent_in if layer == 0 else tangent_mid

        def tangent_step(start, layer=layer, field=field, wide=wide):
            total = summed(field, wide, layer, start)
            lifted = (
                slopes[layer, pl.ds(start * rows, PAIR * rows)]
                * dot(total.astype(jnp.bfloat16), inner_weight[layer], NN)
            ).astype(jnp.bfloat16)
            after = (total + dot(lifted, outer_weight[layer], NN)).reshape(PAIR, rows, features)
            if layer + 1 < layers:
                tangent_mid[pl.ds(start, PAIR)] = after
                tangent_low[pl.ds(start, PAIR)] = after.astype(jnp.bfloat16)
            else:
                cotangent[pl.ds(start, PAIR)] = after
                image[pl.ds(start, PAIR)] = after.astype(jnp.bfloat16)
                for i in range(PAIR):
                    send_image(start + i)

        over_pairs(tangent_step)

    shift.wait_recv()
    final = jnp.logical_and(window == last, group == groups - 1)
    keep = jnp.where(final, 0.0, 1.0)

    def cotangent_step(start):
        here = pl.ds(start, PAIR)
        cotangent[here] = (later[here].astype(jnp.float32) - cotangent[here]) * keep

    over_pairs(cotangent_step)

    adjoint_copies = [
        remote(outgoing.at[peer(d)], adjoint_in.at[window], adjoint_send.at[d], adjoint_recv.at[d], group, peer(d))
        for d in range(1, parts)
    ]
    own = pltpu.make_async_copy(outgoing.at[me], adjoint_in.at[window], local_sem.at[4])

    def send_adjoint(block):
        step = lax.rem(block - me + parts, parts)

        @pl.when(step == 0)
        def _():
            own.start()

        @pl.when(step != 0)
        def _():
            remote(
                outgoing.at[block], adjoint_in.at[window], adjoint_send.at[step], adjoint_recv.at[step], group, block
            ).start()

    for layer in range(layers - 1, -1, -1):

        def adjoint_step(start, layer=layer):
            here = pl.ds(start, PAIR)
            current = cotangent[here].reshape(PAIR * rows, features)
            pulled = (
                slopes[layer, pl.ds(start * rows, PAIR * rows)]
                * dot(current.astype(jnp.bfloat16), outer_weight[layer], NT)
            ).astype(jnp.bfloat16)
            back = (current + dot(pulled, inner_weight[layer], NT)).reshape(PAIR, rows, features)
            returned[here] = back
            returned_low[here] = back.astype(jnp.bfloat16)

        over_pairs(adjoint_step)

        def spread_step(start, layer=layer):
            for i in range(PAIR):
                block = start + i
                above, below = lax.rem(block + 1, parts), lax.rem(block + last, parts)
                stack = jnp.concatenate(
                    [
                        matrix(layer, above)[:, :rows],
                        matrix(layer, block)[:, rows : 2 * rows],
                        matrix(layer, below)[:, 2 * rows :],
                    ],
                    axis=0,
                )
                window = jnp.concatenate([returned_low[above], returned_low[block], returned_low[below]], axis=0)
                after = returned[block] + dot(stack, window, TN)
                if layer > 0:
                    cotangent[block] = after
                else:
                    outgoing[block] = after.astype(jnp.bfloat16)
                    send_adjoint(block)

        over_pairs(spread_step)

    for s in range(parts):
        remote(image.at[0], image_in.at[s], image_send.at[0], image_recv.at[s], group, peer(1)).wait_recv()
    for copy in adjoint_copies:
        copy.wait_recv()
    own.wait()

    for copy in edge_copies + state_copies + inc_copies + [aside, first, second, third, shift] + image_copies[1:]:
        copy.wait_send()
    for copy in adjoint_copies:
        copy.wait_send()

    @pl.when(window == last)
    def _():
        image_copies[0].wait_send()


def local(states, increment, window_slots, edge_weights, inner_weight, inner_bias, outer_weight):
    windows, rows, features = states.shape
    parts = lax.axis_size("mesh")
    groups = lax.axis_size("tm")
    layers, hidden = inner_bias.shape
    if windows != parts or edge_weights.shape[1] != 1 or groups != 4 or parts % PAIR:
        return local_halo(
            states, increment, window_slots, edge_weights, inner_weight, inner_bias, outer_weight
        )
    share = edge_share(window_slots, edge_weights)
    low = pltpu.VMEM((parts, rows, features), jnp.bfloat16)
    wide = pltpu.VMEM((parts, rows, features), jnp.float32)
    sems = pltpu.SemaphoreType.DMA
    vmem, anywhere = pl.BlockSpec(memory_space=pltpu.VMEM), pl.BlockSpec(memory_space=pl.ANY)
    out = jax.ShapeDtypeStruct(increment.shape, jnp.bfloat16)
    image, adjoint = pl.pallas_call(
        functools.partial(whole_kernel, parts),
        out_shape=(out, out),
        in_specs=[anywhere, anywhere, vmem, anywhere, vmem, anywhere],
        out_specs=(anywhere, anywhere),
        scratch_shapes=[
            pltpu.VMEM(inner_weight.shape, jnp.bfloat16),
            pltpu.VMEM(outer_weight.shape, jnp.bfloat16),
            wide, low,
            pltpu.VMEM((groups, 2, parts // 2) + share.shape, jnp.bfloat16),
            low, low, low, low,
            wide, low,
            pltpu.VMEM((layers, parts * rows, hidden), jnp.float32),
            low, wide, wide,
            low, low,
            sems((parts,)), sems((parts,)), sems((parts,)), sems((parts,)), sems((parts,)), sems((parts,)),
            sems((3,)), sems((3,)), sems((1,)), sems((1,)),
            sems((parts,)), sems((parts,)), sems((parts,)), sems((parts,)), sems((5,)),
        ],
        compiler_params=pltpu.CompilerParams(
            collective_id=0, has_side_effects=True, vmem_limit_bytes=56 * 1024 * 1024
        ),
    )(states, increment, share, inner_weight, inner_bias, outer_weight)
    first = jnp.logical_and(lax.axis_index("tm") == 0, jnp.arange(windows)[:, None, None] == 0)
    misfit = increment - jnp.where(first, 0.0, image.astype(jnp.float32))
    return misfit, misfit - adjoint.astype(jnp.float32)


def solution(mesh):
    placed = (
        P("tm", "mesh", None),
        P("tm", "mesh", None),
        P("mesh", None),
        P(None, "mesh", None, None, None),
        P(),
        P(),
        P(),
    )
    return jax.shard_map(
        local,
        mesh=mesh,
        in_specs=placed,
        out_specs=(P("tm", "mesh", None), P("tm", "mesh", None)),
        check_vma=False,
    )
```

```python
import functools

import jax
import jax.numpy as jnp
from jax import lax
from jax.experimental import pallas as pl
from jax.experimental.pallas import tpu as pltpu
from jax.sharding import PartitionSpec as P

LAYERS = 2


HALF_ROOT = 0.7071067811865476
DENSITY_NORM = 0.3989422804014327


def shifted(value, axis, steps):
    count = lax.axis_size(axis)
    pairs = [(source, (source + steps) % count) for source in range(count)]
    return lax.ppermute(value, axis, pairs)


def extended(cells, sides, width):
    for axis, dim in sides:
        count = lax.axis_size(axis)
        head = lax.slice_in_dim(cells, 0, width, axis=dim)
        tail = lax.slice_in_dim(cells, cells.shape[dim] - width, cells.shape[dim], axis=dim)
        cells = jnp.concatenate(
            [
                lax.ppermute(tail, axis, [(i, (i + 1) % count) for i in range(count)]),
                cells,
                lax.ppermute(head, axis, [((i + 1) % count, i) for i in range(count)]),
            ],
            axis=dim,
        )
    return cells


def shifted_2(array, axis, by):
    count = lax.axis_size(axis)
    pairs = [(i, i + by) for i in range(count) if 0 <= i + by < count]
    return lax.ppermute(array, axis, pairs)


def smooth_gate(values):
    return 0.5 * values * (1.0 + lax.erf(values * HALF_ROOT))


def smooth_slope(values):
    return (
        0.5 * (1.0 + lax.erf(values * HALF_ROOT))
        + values * jnp.exp(-0.5 * values * values) * DENSITY_NORM
    )


def aggregate(window, window_slots, weights):
    windows, total_rows, features = window.shape
    blocks = weights.shape[0]
    block_rows = weights.shape[2]
    slots = total_rows // block_rows
    block_view = window.reshape(windows, slots, block_rows, features)
    chosen = (window_slots[:, :, None] == jnp.arange(slots, dtype=jnp.int32)).astype(jnp.float32)
    by_slot = jnp.einsum(
        "bkmn,bkw->bmwn", weights.astype(jnp.float32), chosen, precision=lax.Precision.HIGHEST
    ).astype(jnp.bfloat16)
    summed = jnp.einsum("bmwn,twnd->tbmd", by_slot, block_view, preferred_element_type=jnp.float32)
    return summed.reshape(windows, blocks * block_rows, features)


def transpose_aggregate(source, window_slots, weights):
    windows, node_rows, features = source.shape
    blocks = weights.shape[0]
    block_rows = weights.shape[2]
    block_view = source.reshape(windows, blocks, block_rows, features)
    pieces = jnp.einsum("bkmn,tbmd->tbknd", weights, block_view, preferred_element_type=jnp.float32)
    selector = (
        window_slots[:, :, None] == jnp.arange(blocks + 2, dtype=jnp.int32)[None, None, :]
    ).astype(jnp.float32)
    collected = jnp.einsum("tbknd,bkw->twnd", pieces, selector, precision=lax.Precision.HIGHEST)
    from_right = shifted(collected[:, 0].astype(jnp.bfloat16), "mesh", -1).astype(jnp.float32)
    from_left = shifted(collected[:, blocks + 1].astype(jnp.bfloat16), "mesh", 1).astype(
        jnp.float32
    )
    own_blocks = collected[:, 1 : blocks + 1]
    own_blocks = own_blocks.at[:, 0].add(from_left)
    own_blocks = own_blocks.at[:, blocks - 1].add(from_right)
    return own_blocks.reshape(windows, node_rows, features)


def forward_pass(
    linear_states, source_field, window_slots, edge_weights, inner_weight, inner_bias, outer_weight
):
    windows = linear_states.shape[0]
    block_rows = edge_weights.shape[-1]
    base_state = linear_states
    tangent = source_field
    slopes = []
    for layer_index in range(LAYERS):
        stacked = jnp.concatenate([base_state, tangent.astype(jnp.bfloat16)], axis=0)
        window = extended(stacked, (("mesh", 1),), block_rows)
        blended = aggregate(window, window_slots, edge_weights[layer_index])
        base_sum = base_state.astype(jnp.float32) + blended[:windows]
        tangent_sum = tangent + blended[windows:]
        activation = (
            jnp.einsum(
                "tnd,dh->tnh",
                base_sum.astype(jnp.bfloat16),
                inner_weight[layer_index],
                preferred_element_type=jnp.float32,
            )
            + inner_bias[layer_index]
        )
        derivative = smooth_slope(activation)
        slopes.append(derivative)
        lifted = (
            derivative
            * jnp.einsum(
                "tnd,dh->tnh",
                tangent_sum.astype(jnp.bfloat16),
                inner_weight[layer_index],
                preferred_element_type=jnp.float32,
            )
        ).astype(jnp.bfloat16)
        tangent = tangent_sum + jnp.einsum(
            "tnh,hd->tnd", lifted, outer_weight[layer_index], preferred_element_type=jnp.float32
        )
        if layer_index + 1 < LAYERS:
            gated = smooth_gate(activation).astype(jnp.bfloat16)
            base_state = (
                base_sum
                + jnp.einsum(
                    "tnh,hd->tnd",
                    gated,
                    outer_weight[layer_index],
                    preferred_element_type=jnp.float32,
                )
            ).astype(jnp.bfloat16)
    return (slopes, tangent)


def adjoint_pass(slopes, cotangent, window_slots, edge_weights, inner_weight, outer_weight):
    current = cotangent
    for layer_index in range(LAYERS - 1, -1, -1):
        narrow = current.astype(jnp.bfloat16)
        spread = jnp.einsum(
            "tnd,hd->tnh", narrow, outer_weight[layer_index], preferred_element_type=jnp.float32
        )
        pulled = (slopes[layer_index] * spread).astype(jnp.bfloat16)
        returned = current + jnp.einsum(
            "tnh,dh->tnd", pulled, inner_weight[layer_index], preferred_element_type=jnp.float32
        )
        current = returned + transpose_aggregate(
            returned.astype(jnp.bfloat16), window_slots, edge_weights[layer_index]
        )
    return current


def local_halo(states, increment, window_slots, edge_weights, inner_weight, inner_bias, outer_weight):
    windows = states.shape[0]
    kept_slopes, images = forward_pass(
        states, increment, window_slots, edge_weights, inner_weight, inner_bias, outer_weight
    )
    previous = shifted_2(images[windows - 1 :].astype(jnp.bfloat16), "tm", 1).astype(jnp.float32)
    misfit = increment - jnp.concatenate([previous, images[: windows - 1]], axis=0)
    following = shifted_2(misfit[:1].astype(jnp.bfloat16), "tm", -1).astype(jnp.float32)
    cotangent = jnp.concatenate([misfit[1:], following], axis=0)
    pulled_back = adjoint_pass(
        kept_slopes, cotangent, window_slots, edge_weights, inner_weight, outer_weight
    )
    normal = misfit - pulled_back
    return (misfit, normal)


def edge_share(window_slots, edge_weights):
    names = jnp.arange(3, dtype=jnp.int32)
    chosen = (window_slots[0][:, None] == names[None, :]).astype(jnp.float32)
    summed = jnp.einsum(
        "lkmn,ks->lmsn", edge_weights[:, 0].astype(jnp.float32), chosen, precision=lax.Precision.HIGHEST
    ).astype(jnp.bfloat16)
    layers, rows, slots, columns = summed.shape
    share = rows // lax.axis_size("tm")
    mine = lax.dynamic_slice_in_dim(summed, lax.axis_index("tm") * share, share, axis=1)
    return mine.reshape(layers, share, slots * columns)


def dot(left, right, dims):
    return lax.dot_general(left, right, (dims, ((), ())), preferred_element_type=jnp.float32)


NN = ((1,), (0,))
NT = ((1,), (1,))
TN = ((0,), (0,))
PAIR = 4


def whole_kernel(
    parts, states, increment, share, inner_hbm, inner_bias, outer_hbm, image_in, adjoint_in,
    inner_weight, outer_weight, wide_in, narrow, edges, base, tangent_in, later, base_next, tangent_mid, tangent_low, slopes, image, cotangent, returned,
    returned_low, outgoing,
    edge_send, edge_recv, state_send, state_recv, inc_send, inc_recv, tm_send, tm_recv, shift_send, shift_recv,
    image_send, image_recv, adjoint_send, adjoint_recv, local_sem,
):
    group, me = lax.axis_index("tm"), lax.axis_index("mesh")
    groups = lax.axis_size("tm")
    last = parts - 1
    layers = inner_weight.shape[0]
    rows, features = base.shape[1], base.shape[2]
    group_next, group_prev = lax.rem(group + 1, groups), lax.rem(group + groups - 1, groups)
    across = lax.rem(group + 2, groups)
    beside = group + 1 - 2 * lax.rem(group, 2)
    beside_across = lax.rem(beside + 2, groups)

    pairs = parts // 2
    high, side = me // 2, lax.rem(me, 2)

    def window_of(g, m):
        order = jnp.where(lax.rem(m, 2) == 0, m // 2, parts - 1 - m // 2)
        return jnp.where(lax.rem(g, 2) == 0, order, last - order)

    def holder_of(g, w):
        order = jnp.where(lax.rem(g, 2) == 0, w, last - w)
        return jnp.where(order < pairs, 2 * order, 2 * (last - order) + 1)

    window = window_of(group, me)
    prev_last, next_first = holder_of(group_prev, last), holder_of(group_next, 0)

    def peer(step):
        return lax.rem(me + step, parts)

    barrier = pltpu.get_barrier_semaphore()

    def greet(g, m):
        pl.semaphore_signal(barrier, inc=1, device_id={"tm": g, "mesh": m}, device_id_type=pl.DeviceIdType.MESH)

    for step in range(1, parts):
        greet(group, peer(step))
    greet(across, me)
    greet(beside, me)
    greet(group_prev, prev_last)

    @pl.when(window == last)
    def _():
        greet(group_next, next_first)

    pl.semaphore_wait(
        barrier, parts + 1 + jnp.where(window == last, parts, 0) + jnp.where(window == 0, 1, 0)
    )

    def remote(src, dst, send, recv, g, m):
        return pltpu.make_async_remote_copy(
            src_ref=src, dst_ref=dst, send_sem=send, recv_sem=recv,
            device_id={"tm": g, "mesh": m}, device_id_type=pl.DeviceIdType.MESH,
        )

    edge_copies = [
        remote(share, edges.at[group, side, high], edge_send.at[d], edge_recv.at[d], group, peer(2 * d))
        for d in range(1, pairs)
    ]
    state_copies = [
        remote(states.at[window_of(group, peer(d))], base.at[me], state_send.at[d], state_recv.at[d], group, peer(d))
        for d in range(1, parts)
    ]
    inc_copies = [
        remote(narrow.at[window_of(group, peer(d))], tangent_in.at[me], inc_send.at[d], inc_recv.at[d], group, peer(d))
        for d in range(1, parts)
    ]
    fetch = pltpu.make_async_copy(increment, wide_in, local_sem.at[0])
    loads = [
        pltpu.make_async_copy(inner_hbm, inner_weight, local_sem.at[1]),
        pltpu.make_async_copy(outer_hbm, outer_weight, local_sem.at[2]),
        pltpu.make_async_copy(states.at[window], base.at[me], local_sem.at[3]),
    ]
    fetch.start()
    for copy in edge_copies + state_copies:
        copy.start()
    fetch.wait()
    narrow[...] = wide_in[...].astype(jnp.bfloat16)
    for copy in inc_copies + loads:
        copy.start()
    edges[group, side, high] = share[...]
    tangent_in[me] = narrow[window]
    for copy in edge_copies:
        copy.wait_recv()
    aside = remote(
        edges.at[group, side], edges.at[group, side], edge_send.at[0], edge_recv.at[0], group, me + 1 - 2 * side
    )
    aside.start()
    aside.wait_recv()
    first = remote(edges.at[group], edges.at[group], tm_send.at[0], tm_recv.at[0], across, me)
    first.start()
    second = remote(edges.at[group], edges.at[group], tm_send.at[1], tm_recv.at[1], beside, me)
    second.start()
    first.wait_recv()
    third = remote(edges.at[across], edges.at[across], tm_send.at[2], tm_recv.at[2], beside, me)
    third.start()
    second.wait_recv()
    third.wait_recv()
    for copy in loads:
        copy.wait()
    for copy in state_copies:
        copy.wait_recv()

    def matrix(layer, block):
        return edges[:, lax.rem(block, 2), block // 2, layer].reshape(rows, -1)

    def aggregated(field, layer, block):
        window = jnp.concatenate(
            [field[lax.rem(block + last, parts)], field[block], field[lax.rem(block + 1, parts)]], axis=0
        )
        return dot(matrix(layer, block), window, NN)

    def summed(field, wide, layer, start):
        parts_of = [wide[start + i].astype(jnp.float32) + aggregated(field, layer, start + i) for i in range(PAIR)]
        return jnp.concatenate(parts_of, axis=0)

    def over_pairs(body):
        def step(index, carry):
            body(lax.rem(index + me // PAIR, parts // PAIR) * PAIR)
            return carry

        lax.fori_loop(0, parts // PAIR, step, 0)

    for layer in range(layers):
        field = base if layer == 0 else base_next

        def base_step(start, layer=layer, field=field):
            total = summed(field, field, layer, start)
            pre = dot(total.astype(jnp.bfloat16), inner_weight[layer], NN) + inner_bias[layer][None, :]
            phi = 0.5 * (1.0 + lax.erf(pre * HALF_ROOT))
            slopes[layer, pl.ds(start * rows, PAIR * rows)] = (
                phi + pre * jnp.exp(-0.5 * pre * pre) * DENSITY_NORM
            )
            if layer + 1 < layers:
                after = total + dot((pre * phi).astype(jnp.bfloat16), outer_weight[layer], NN)
                base_next[pl.ds(start, PAIR)] = after.astype(jnp.bfloat16).reshape(PAIR, rows, features)

        over_pairs(base_step)

    for copy in inc_copies:
        copy.wait_recv()
    low_group = jnp.where(window == 0, group_prev, group)
    low_me = jnp.where(window == 0, prev_last, holder_of(group, lax.rem(window + last, parts)))
    shift = remote(tangent_in, later, shift_send.at[0], shift_recv.at[0], low_group, low_me)
    shift.start()

    slot = lax.rem(window + 1, parts)
    own_group = jnp.where(window == last, group_next, group)
    image_copies = [
        remote(image.at[peer(d)], image_in.at[slot], image_send.at[d], image_recv.at[slot], own_group, peer(d))
        for d in range(parts)
    ]
    kept = pltpu.make_async_copy(image.at[me], image_in.at[slot], image_recv.at[slot])

    def send_image(block):
        step = lax.rem(block - me + parts, parts)
        stays = jnp.logical_and(step == 0, window != last)

        @pl.when(stays)
        def _():
            kept.start()

        @pl.when(jnp.logical_not(stays))
        def _():
            remote(
                image.at[block], image_in.at[slot], image_send.at[step], image_recv.at[slot], own_group, block
            ).start()

    for layer in range(layers):
        field = tangent_in if layer == 0 else tangent_low
        wide = tangent_in if layer == 0 else tangent_mid

        def tangent_step(start, layer=layer, field=field, wide=wide):
            total = summed(field, wide, layer, start)
            lifted = (
                slopes[layer, pl.ds(start * rows, PAIR * rows)]
                * dot(total.astype(jnp.bfloat16), inner_weight[layer], NN)
            ).astype(jnp.bfloat16)
            after = (total + dot(lifted, outer_weight[layer], NN)).reshape(PAIR, rows, features)
            if layer + 1 < layers:
                tangent_mid[pl.ds(start, PAIR)] = after
                tangent_low[pl.ds(start, PAIR)] = after.astype(jnp.bfloat16)
            else:
                cotangent[pl.ds(start, PAIR)] = after
                image[pl.ds(start, PAIR)] = after.astype(jnp.bfloat16)
                for i in range(PAIR):
                    send_image(start + i)

        over_pairs(tangent_step)

    shift.wait_recv()
    final = jnp.logical_and(window == last, group == groups - 1)
    keep = jnp.where(final, 0.0, 1.0)

    def cotangent_step(start):
        here = pl.ds(start, PAIR)
        cotangent[here] = (later[here].astype(jnp.float32) - cotangent[here]) * keep

    over_pairs(cotangent_step)

    adjoint_copies = [
        remote(outgoing.at[peer(d)], adjoint_in.at[window], adjoint_send.at[d], adjoint_recv.at[d], group, peer(d))
        for d in range(1, parts)
    ]
    own = pltpu.make_async_copy(outgoing.at[me], adjoint_in.at[window], local_sem.at[4])

    def send_adjoint(block):
        step = lax.rem(block - me + parts, parts)

        @pl.when(step == 0)
        def _():
            own.start()

        @pl.when(step != 0)
        def _():
            remote(
                outgoing.at[block], adjoint_in.at[window], adjoint_send.at[step], adjoint_recv.at[step], group, block
            ).start()

    for layer in range(layers - 1, -1, -1):

        def adjoint_step(start, layer=layer):
            here = pl.ds(start, PAIR)
            current = cotangent[here].reshape(PAIR * rows, features)
            pulled = (
                slopes[layer, pl.ds(start * rows, PAIR * rows)]
                * dot(current.astype(jnp.bfloat16), outer_weight[layer], NT)
            ).astype(jnp.bfloat16)
            back = (current + dot(pulled, inner_weight[layer], NT)).reshape(PAIR, rows, features)
            returned[here] = back
            returned_low[here] = back.astype(jnp.bfloat16)

        over_pairs(adjoint_step)

        def spread_step(start, layer=layer):
            for i in range(PAIR):
                block = start + i
                above, below = lax.rem(block + 1, parts), lax.rem(block + last, parts)
                stack = jnp.concatenate(
                    [
                        matrix(layer, above)[:, :rows],
                        matrix(layer, block)[:, rows : 2 * rows],
                        matrix(layer, below)[:, 2 * rows :],
                    ],
                    axis=0,
                )
                window = jnp.concatenate([returned_low[above], returned_low[block], returned_low[below]], axis=0)
                after = returned[block] + dot(stack, window, TN)
                if layer > 0:
                    cotangent[block] = after
                else:
                    outgoing[block] = after.astype(jnp.bfloat16)
                    send_adjoint(block)

        over_pairs(spread_step)

    for s in range(parts):
        remote(image.at[0], image_in.at[s], image_send.at[0], image_recv.at[s], group, peer(1)).wait_recv()
    for copy in adjoint_copies:
        copy.wait_recv()
    own.wait()

    for copy in edge_copies + state_copies + inc_copies + [aside, first, second, third, shift] + image_copies[1:]:
        copy.wait_send()
    for copy in adjoint_copies:
        copy.wait_send()

    @pl.when(window == last)
    def _():
        image_copies[0].wait_send()


def local(states, increment, window_slots, edge_weights, inner_weight, inner_bias, outer_weight):
    windows, rows, features = states.shape
    parts = lax.axis_size("mesh")
    groups = lax.axis_size("tm")
    layers, hidden = inner_bias.shape
    if windows != parts or edge_weights.shape[1] != 1 or groups != 4 or parts % PAIR:
        return local_halo(
            states, increment, window_slots, edge_weights, inner_weight, inner_bias, outer_weight
        )
    share = edge_share(window_slots, edge_weights)
    low = pltpu.VMEM((parts, rows, features), jnp.bfloat16)
    wide = pltpu.VMEM((parts, rows, features), jnp.float32)
    sems = pltpu.SemaphoreType.DMA
    vmem, anywhere = pl.BlockSpec(memory_space=pltpu.VMEM), pl.BlockSpec(memory_space=pl.ANY)
    out = jax.ShapeDtypeStruct(increment.shape, jnp.bfloat16)
    image, adjoint = pl.pallas_call(
        functools.partial(whole_kernel, parts),
        out_shape=(out, out),
        in_specs=[anywhere, anywhere, vmem, anywhere, vmem, anywhere],
        out_specs=(anywhere, anywhere),
        scratch_shapes=[
            pltpu.VMEM(inner_weight.shape, jnp.bfloat16),
            pltpu.VMEM(outer_weight.shape, jnp.bfloat16),
            wide, low,
            pltpu.VMEM((groups, 2, parts // 2) + share.shape, jnp.bfloat16),
            low, low, low, low,
            wide, low,
            pltpu.VMEM((layers, parts * rows, hidden), jnp.float32),
            low, wide, wide,
            low, low,
            sems((parts,)), sems((parts,)), sems((parts,)), sems((parts,)), sems((parts,)), sems((parts,)),
            sems((3,)), sems((3,)), sems((1,)), sems((1,)),
            sems((parts,)), sems((parts,)), sems((parts,)), sems((parts,)), sems((5,)),
        ],
        compiler_params=pltpu.CompilerParams(
            collective_id=0, has_side_effects=True, vmem_limit_bytes=56 * 1024 * 1024
        ),
    )(states, increment, share, inner_weight, inner_bias, outer_weight)
    first = jnp.logical_and(lax.axis_index("tm") == 0, jnp.arange(windows)[:, None, None] == 0)
    misfit = increment - jnp.where(first, 0.0, image.astype(jnp.float32))
    return misfit, misfit - adjoint.astype(jnp.float32)


def solution(mesh):
    placed = (
        P("tm", "mesh", None),
        P("tm", "mesh", None),
        P("mesh", None),
        P(None, "mesh", None, None, None),
        P(),
        P(),
        P(),
    )
    return jax.shard_map(
        local,
        mesh=mesh,
        in_specs=placed,
        out_specs=(P("tm", "mesh", None), P("tm", "mesh", None)),
        check_vma=False,
    )
```
